32 devices in a mesh: groups: 2 (over x), space: 16 (over z, y, core).
Axes of the slice: x: 2, y: 2, z: 4, core: 2. Of those that a mesh axis runs over, the one named last changes fastest.
Arguments:
- features: bfloat16 [4096, 4, 128], P(('groups', 'space')), parts along dimension 0, may hold values from -6 to 6
- positions: float32 [3, 4096], P(None, ('groups', 'space')), parts along dimension 1, may hold values from -8 to 8
- species: int32 [4096], P(('groups', 'space')), parts along dimension 0, may hold values from 0 to 88
- block_pair_table: int32 [2, 64], P(None, ('groups', 'space')), parts along dimension 1, may hold values from 0 to 15, as said below
- device_pair_count: int32 [32], P(('groups', 'space')), parts along dimension 0, may hold values from 1 to 2, as said below
- edge_tile_masks: int32 [64, 128, 128], P(('groups', 'space')), parts along dimension 0, may hold values 0 or 1
- radial: float32 [4, 8, 128], replicated, may hold values from -0.6 to 0.6
- element_scale_table: float32 [89, 128], replicated, may hold values from 0.1 to 1.9
- linear_mixing_weight: bfloat16 [128, 128], replicated, may hold values from -0.5 to 0.5
- down_adapter_weight: bfloat16 [128, 16], replicated, may hold values from -0.5 to 0.5
- up_adapter_weight: bfloat16 [16, 128], replicated, may hold values from -1.5 to 1.5
- readout_weight: float32 [128], replicated, may hold values from -0.5 to 0.5
- atom_energy_weight: float32 [4096], P(('groups', 'space')), parts along dimension 0, may hold values from -6 to 6
Outputs:
- energies: float32 [4096], P(('groups', 'space')), parts along dimension 0
- coordinate_gradient: float32 [3, 4096], P(None, ('groups', 'space')), parts along dimension 1
- down_adapter_gradient: float32 [256, 16], P('groups'), parts along dimension 0
- up_adapter_gradient: float32 [32, 128], P('groups'), parts along dimension 0
The draws below stay inside these ranges and needn't reach their ends.
There are 2 independent parts, one for each index of `groups`. The reference program is written for one: setup_inputs(seed, part) draws one part's arguments, and reference() takes and returns one part's arrays. A program takes and returns all parts, laid end to end along the dimension named above; an argument that names none is the same for every part. Nothing has to cross between parts.
Inputs may be any that keep to these rules, and one draw needn't show every extreme that they name: `block_pair_table`: every slot's receiver and sender blocks lie within 2 devices of the slot's device along the wrapped axis (block c is homed on device c); distance 2 occurs on every device. Slots of a device at index device_pair_count or above are unused; some device uses all 2.
All inputs are finite; a program needn't handle non-finite values. No bound on the sum of `edge_tile_masks` on one device may be relied on, other than what follows from the above.
Results may differ from the reference program's by a relative error of at most 0.003.
The reference program's roundings to bfloat16 on the way count: a program that leaves them out, or rounds other values in their place, can miss the bound.
Values may be sent and summed in bfloat16 or wider, within the bound.
A program may use at most 64 MiB of HBM per device.

```python
import math
import jax
import jax.numpy as jnp
import numpy as np
from jax import lax

FEATURE_CHANNELS = 128
NSPEC = 89
ATOMS = 128
KRAD = 8
ADAPTER_RANK = 16
REACH = 2
PAIR_DEV = 2
BLOCKS = 16
NATOM = 2048
PAIRS = 32


def draw_block_pair_table(key, part):
    key = jax.random.fold_in(key, 11)
    slot_ids = jnp.arange(PAIR_DEV * BLOCKS, dtype=jnp.int32)
    home_device = slot_ids // PAIR_DEV
    shifts = jax.random.randint(key, (2, PAIR_DEV * BLOCKS), -REACH, REACH + 1, dtype=jnp.int32)
    first_slot = slot_ids % PAIR_DEV == 0
    extremes = jnp.array([[-REACH], [REACH]], dtype=jnp.int32)
    shifts = jnp.where(first_slot[None, :], extremes, shifts)
    return ((home_device[None, :] + shifts) % BLOCKS).astype(jnp.int32)


def draw_device_pair_count(key, part):
    key = jax.random.fold_in(key, 12)
    counts = jax.random.randint(jax.random.fold_in(key, 1), (BLOCKS,), 1, PAIR_DEV + 1, dtype=jnp.int32)
    full_device = jax.random.randint(jax.random.fold_in(key, 2), (), 0, BLOCKS, dtype=jnp.int32)
    return jnp.where(jnp.arange(BLOCKS, dtype=jnp.int32) == full_device, PAIR_DEV, counts).astype(jnp.int32)


def touch_ends(values, own_key, low, largest):
    place = [jax.random.randint(jax.random.fold_in(own_key, axis), (), 0, length) for axis, length in enumerate(values.shape)]
    widest = values.shape.index(max(values.shape))
    next_to = place[:widest] + [(place[widest] + 1) % values.shape[widest]] + place[widest + 1:]
    return values.at[tuple(place)].set(low).at[tuple(next_to)].set(largest)


def shard_levels(own_key, extent, shards, least, largest):
    level = 1.0
    for dim, shards_of in shards:
        steps = jax.random.uniform(jax.random.fold_in(jax.random.fold_in(own_key, 6), dim), (shards_of,), jnp.float32, least / len(shards), largest / len(shards))
        level = level * jnp.repeat(jnp.exp(steps), extent[dim] // shards_of).reshape((-1,) + (1,) * (len(extent) - 1 - dim))
    return level


def cumulative_ranks(number_of, lean):
    portions = [(1 << 20) // math.isqrt(grade ** lean) + 1 for grade in range(1, number_of + 1)]
    scale = 1 + sum(portions) // (1 << 30)
    return np.cumsum(np.array([max(1, weight // scale) for weight in portions]))


def ranked_ids(rng, dims, number_of, lean):
    table = cumulative_ranks(number_of, lean)
    lot = jax.random.randint(jax.random.fold_in(rng, 1), dims, 0, int(table[number_of - 1]))
    standing = jnp.searchsorted(jnp.asarray(table, jnp.int32), lot, side="right")
    return jax.random.permutation(jax.random.fold_in(rng, 2), number_of)[standing].astype(jnp.int32)


def noise(key, extent, scale, bound, pieces=(), kind=jnp.bfloat16):
    factor_of = shard_levels(key, extent, pieces, -0.22, 0.18) if pieces else 1.0
    drawn = jax.random.normal(key, extent, jnp.float32) * scale * factor_of
    return jnp.minimum(jnp.maximum(drawn, -bound), bound).astype(kind)


def setup_inputs(seed: int = 0, part: int = 0) -> dict:
    arg_keys = jax.random.split(jax.random.key(seed), 14)
    own_keys = jax.random.split(jax.random.fold_in(arg_keys[13], part), 14)
    features = noise(own_keys[0], (NATOM, 4, FEATURE_CHANNELS), 1.0, 6.0, ((0, 16),))
    positions = noise(own_keys[1], (3, NATOM), 2.0, 8.0, ((1, 16),), jnp.float32)
    species = touch_ends(ranked_ids(own_keys[2], (NATOM,), NSPEC, 2), jax.random.fold_in(own_keys[2], 3), 0, NSPEC - 1).astype(jnp.int32)
    block_pair_table = draw_block_pair_table(jax.random.fold_in(jax.random.fold_in(arg_keys[13], part), 71), part)
    device_pair_count = draw_device_pair_count(jax.random.fold_in(jax.random.fold_in(arg_keys[13], part), 71), part)
    edge_tile_masks = touch_ends((jax.random.randint(own_keys[5], (PAIRS, ATOMS, ATOMS), 0, 3) < 1).astype(jnp.int32), jax.random.fold_in(own_keys[5], 1), 0, 1)
    radial = noise(arg_keys[6], (4, KRAD, FEATURE_CHANNELS), 0.1, 0.6, (), jnp.float32)
    element_scale_table = jnp.clip(1.0 + 0.18 * jax.random.normal(arg_keys[7], (NSPEC, FEATURE_CHANNELS), jnp.float32), 0.1, 1.9)
    linear_mixing_weight = noise(arg_keys[8], (FEATURE_CHANNELS, FEATURE_CHANNELS), FEATURE_CHANNELS ** -0.5, 0.5)
    down_adapter_weight = noise(arg_keys[9], (FEATURE_CHANNELS, ADAPTER_RANK), FEATURE_CHANNELS ** -0.5, 0.5)
    up_adapter_weight = noise(arg_keys[10], (ADAPTER_RANK, FEATURE_CHANNELS), ADAPTER_RANK ** -0.5, 1.5)
    readout_weight = noise(arg_keys[11], (FEATURE_CHANNELS,), FEATURE_CHANNELS ** -0.5, 0.5, (), jnp.float32)
    atom_energy_weight = noise(own_keys[12], (NATOM,), 1.0, 6.0, ((0, 16),), jnp.float32)
    return {"features": features, "positions": positions, "species": species, "block_pair_table": block_pair_table, "device_pair_count": device_pair_count, "edge_tile_masks": edge_tile_masks, "radial": radial, "element_scale_table": element_scale_table, "linear_mixing_weight": linear_mixing_weight, "down_adapter_weight": down_adapter_weight, "up_adapter_weight": up_adapter_weight, "readout_weight": readout_weight, "atom_energy_weight": atom_energy_weight}


soft_core = 0.25
centre_start = 1.0
centre_step = 1.0
basis_width = 1.0
highest = lax.Precision.HIGHEST

def geometry(recv_pos, send_pos):
    offsets = send_pos[None, :, :] - jnp.transpose(recv_pos)[:, :, None]
    distance = jnp.sqrt(lax.optimization_barrier(jnp.sum(offsets * offsets, axis=1)) + soft_core)
    unit_dir = offsets / distance[:, None, :]
    return (distance, unit_dir)

def feature_views(send_feat):
    atom_count = send_feat.shape[0]
    channels = send_feat.shape[2]
    flat_feat = send_feat.reshape(atom_count, 4 * channels)
    scalars = send_feat[:, 0, :]
    vec_stack = jnp.transpose(send_feat[:, 1:, :], (1, 0, 2)).reshape(3 * atom_count, channels)
    return (flat_feat, scalars, vec_stack)

def radial_bump(distance, basis_index):
    scaled = (distance - (centre_start + centre_step * basis_index)) / basis_width
    return (scaled, jnp.exp(-scaled * scaled))

def contract_trailing(left, right):
    return lax.dot_general(left, right, (((1,), (1,)), ((), ())), preferred_element_type=jnp.float32)

def contract_first(left, right):
    return lax.dot_general(left, right, (((0,), (0,)), ((), ())), preferred_element_type=jnp.float32)

def tile_messages(recv_pos, send_pos, edge_mask, send_feat, radial):
    atom_count = send_feat.shape[0]
    channels = send_feat.shape[2]
    distance, unit_dir = geometry(recv_pos, send_pos)
    mask_float = edge_mask.astype(jnp.float32)
    flat_feat, scalars, vec_stack = feature_views(send_feat)
    scal_msg = jnp.zeros((atom_count, channels), jnp.float32)
    vec_msg = jnp.zeros((atom_count, 3, channels), jnp.float32)
    for basis_index in range(radial.shape[1]):
        scaled, bump_value = radial_bump(distance, basis_index)
        masked = bump_value * mask_float
        plain_tile = masked.astype(jnp.bfloat16)
        dir_tile = (masked[:, None, :] * unit_dir).astype(jnp.bfloat16)
        product_all = jnp.dot(plain_tile, flat_feat, preferred_element_type=jnp.float32)
        along_dir = jnp.dot(dir_tile.reshape(3 * atom_count, atom_count), scalars, preferred_element_type=jnp.float32).reshape(atom_count, 3, channels)
        inner_dot = jnp.dot(dir_tile.reshape(atom_count, 3 * atom_count), vec_stack, preferred_element_type=jnp.float32)
        scal_msg = scal_msg + radial[0, basis_index] * product_all[:, :channels] + radial[1, basis_index] * inner_dot
        vec_msg = vec_msg + radial[2, basis_index] * along_dir + radial[3, basis_index] * product_all[:, channels:].reshape(atom_count, 3, channels)
    return jnp.concatenate([scal_msg[:, None, :], vec_msg], axis=1)

def tile_gradients(recv_pos, send_pos, edge_mask, send_feat, radial, backward_seed):
    atom_count = send_feat.shape[0]
    channels = send_feat.shape[2]
    distance, unit_dir = geometry(recv_pos, send_pos)
    mask_float = edge_mask.astype(jnp.float32)
    flat_feat, scalars, vec_stack = feature_views(send_feat)
    cot_scalar = backward_seed[:, 0, :]
    cot_vector = backward_seed[:, 1:, :]
    grad_dist = jnp.zeros((atom_count, atom_count), jnp.float32)
    grad_unit = jnp.zeros((atom_count, 3, atom_count), jnp.float32)
    for basis_index in range(radial.shape[1]):
        scaled, bump_value = radial_bump(distance, basis_index)
        masked = bump_value * mask_float
        weighted_all = jnp.concatenate([radial[0, basis_index] * cot_scalar, (radial[3, basis_index] * cot_vector).reshape(atom_count, 3 * channels)], axis=1).astype(jnp.bfloat16)
        grad_plain = contract_trailing(weighted_all, flat_feat)
        weighted_along = (radial[2, basis_index] * cot_vector).reshape(3 * atom_count, channels).astype(jnp.bfloat16)
        weighted_inner = (radial[1, basis_index] * cot_scalar).astype(jnp.bfloat16)
        grad_dir = contract_trailing(weighted_along, scalars).reshape(atom_count, 3, atom_count) + contract_trailing(weighted_inner, vec_stack).reshape(atom_count, 3, atom_count)
        grad_bump = mask_float * (grad_plain + lax.optimization_barrier(jnp.sum(grad_dir * unit_dir, axis=1)))
        grad_dist = grad_dist + grad_bump * bump_value * (-2.0 * scaled / basis_width)
        grad_unit = grad_unit + masked[:, None, :] * grad_dir
    radial_part = lax.optimization_barrier(jnp.sum(grad_unit * unit_dir, axis=1))
    grad_offset = grad_dist[:, None, :] * unit_dir + (grad_unit - unit_dir * radial_part[:, None, :]) / distance[:, None, :]
    recv_grad = -jnp.transpose(lax.optimization_barrier(jnp.sum(grad_offset, axis=2)))
    send_grad = lax.optimization_barrier(jnp.sum(grad_offset, axis=0))
    return (recv_grad, send_grad)

def species_scale(species, element_scale_table):
    one_hot = (species[:, None] == jnp.arange(element_scale_table.shape[0], dtype=jnp.int32)[None, :]).astype(jnp.float32)
    return jnp.dot(one_hot, element_scale_table, precision=highest, preferred_element_type=jnp.float32)

def atom_update(gather_messages, scale_factor, linear_mixing_weight, down_adapter_weight, up_adapter_weight):
    invariant = scale_factor * (gather_messages[:, 0, :] + lax.optimization_barrier(jnp.sum(gather_messages[:, 1:, :] * gather_messages[:, 1:, :], axis=1)))
    invariant_second = invariant.astype(jnp.bfloat16)
    reduced_features = jnp.dot(invariant_second, down_adapter_weight, preferred_element_type=jnp.float32).astype(jnp.bfloat16)
    hidden_preactivation = jnp.dot(invariant_second, linear_mixing_weight, preferred_element_type=jnp.float32) + jnp.dot(reduced_features, up_adapter_weight, preferred_element_type=jnp.float32)
    return (invariant_second, reduced_features, hidden_preactivation)

def atom_update_backward(gather_messages, scale_factor, invariant_second, reduced_features, hidden_preactivation, linear_mixing_weight, down_adapter_weight, up_adapter_weight, readout_weight, atom_energy_weight):
    sigma = jax.nn.sigmoid(hidden_preactivation)
    slope = sigma * (1.0 + hidden_preactivation * (1.0 - sigma))
    preactivation_gradient = (atom_energy_weight[:, None] * readout_weight[None, :] * slope).astype(jnp.bfloat16)
    second_summand = contract_first(reduced_features, preactivation_gradient)
    reduced_gradient = contract_trailing(preactivation_gradient, up_adapter_weight).astype(jnp.bfloat16)
    first_summand = contract_first(invariant_second, reduced_gradient)
    invariant_gradient = contract_trailing(preactivation_gradient, linear_mixing_weight) + contract_trailing(reduced_gradient, down_adapter_weight)
    grad_scalar = scale_factor * invariant_gradient
    backward_seed = jnp.concatenate([grad_scalar[:, None, :], 2.0 * grad_scalar[:, None, :] * gather_messages[:, 1:, :]], axis=1)
    return (backward_seed, first_summand, second_summand)

def reference(features, positions, species, block_pair_table, device_pair_count, edge_tile_masks, radial, element_scale_table, linear_mixing_weight, down_adapter_weight, up_adapter_weight, readout_weight, atom_energy_weight):
    block_total = features.shape[0] // ATOMS
    feat_blocks = features.reshape(block_total, ATOMS, 4, FEATURE_CHANNELS)
    pos_blocks = jnp.transpose(positions.reshape(3, block_total, ATOMS), (1, 0, 2))
    slot_total = block_pair_table.shape[1]
    slot_ids = jnp.arange(slot_total, dtype=jnp.int32)
    live = (slot_ids % PAIR_DEV < device_pair_count[slot_ids // PAIR_DEV]).astype(jnp.float32)
    receiver = block_pair_table[0]
    sender = block_pair_table[1]

    def add_message(total, index):
        message = tile_messages(pos_blocks[receiver[index]], pos_blocks[sender[index]], edge_tile_masks[index], feat_blocks[sender[index]], radial)
        return (total.at[receiver[index]].add(message * live[index]), None)
    gather_messages = lax.scan(add_message, jnp.zeros((block_total, ATOMS, 4, FEATURE_CHANNELS), jnp.float32), slot_ids)[0]
    gather_messages = gather_messages.reshape(block_total * ATOMS, 4, FEATURE_CHANNELS)
    scale_factor = species_scale(species, element_scale_table)
    invariant_second, reduced_features, hidden_preactivation = atom_update(gather_messages, scale_factor, linear_mixing_weight, down_adapter_weight, up_adapter_weight)
    energies = jnp.dot(jax.nn.silu(hidden_preactivation), readout_weight, precision=highest, preferred_element_type=jnp.float32)
    backward_seed, down_adapter_gradient, up_adapter_gradient = atom_update_backward(gather_messages, scale_factor, invariant_second, reduced_features, hidden_preactivation, linear_mixing_weight, down_adapter_weight, up_adapter_weight, readout_weight, atom_energy_weight)
    cot_blocks = backward_seed.reshape(block_total, ATOMS, 4, FEATURE_CHANNELS)

    def add_gradient(total, index):
        recv_grad, send_grad = tile_gradients(pos_blocks[receiver[index]], pos_blocks[sender[index]], edge_tile_masks[index], feat_blocks[sender[index]], radial, cot_blocks[receiver[index]])
        total = total.at[receiver[index]].add(recv_grad * live[index])
        total = total.at[sender[index]].add(send_grad * live[index])
        return (total, None)
    grad_blocks = lax.scan(add_gradient, jnp.zeros((block_total, 3, ATOMS), jnp.float32), slot_ids)[0]
    coordinate_gradient = jnp.transpose(grad_blocks, (1, 0, 2)).reshape(3, block_total * ATOMS)
    return (energies, coordinate_gradient, down_adapter_gradient, up_adapter_gradient)
```

```python
import functools

import jax
import jax.numpy as jnp
from jax import lax
from jax.experimental import pallas as pl
from jax.experimental.pallas import tpu as pltpu
from jax.sharding import PartitionSpec as P

REACH = 2
WINDOW = 2 * REACH + 1

soft_core = 0.25
centre_start = 1.0
highest = lax.Precision.HIGHEST
MESH = pl.DeviceIdType.MESH
f32 = jnp.float32
bf16 = jnp.bfloat16


def dot(left, right):
    return jnp.dot(left, right, preferred_element_type=f32)


def dot_trailing(left, right):
    return lax.dot_general(left, right, (((1,), (1,)), ((), ())), preferred_element_type=f32)


def kernel(
    count,
    rounds,
    table_ref,
    live_ref,
    feat_ref,
    pos_ref,
    species_ref,
    mask_ref,
    radial_ref,
    scale_ref,
    mix_ref,
    down_ref,
    up_ref,
    readout_ref,
    weight_ref,
    energy_ref,
    coord_ref,
    down_grad_ref,
    up_grad_ref,
    feat_win,
    cot_win,
    pos_win,
    partial,
    sib_out,
    sib_in,
    far_out,
    far_in,
    near_out,
    near_in,
    lefts,
    masked_buf,
    dist_buf,
    unit_buf,
    acc,
    grad_dist,
    grad_unit,
    scale_buf,
    table_pad,
    grad_out,
    grad_in,
    ring_out,
    ring_in,
    feat_send,
    feat_recv,
    cot_send,
    cot_recv,
    pos_send,
    pos_recv,
    msg_send,
    msg_recv,
    grad_send,
    grad_recv,
    ring_send,
    ring_recv,
):
    comps, atoms, channels = feat_ref.shape
    slots = mask_ref.shape[0]
    basis = radial_ref.shape[1]
    me = lax.axis_index("space")
    core = lax.rem(me, 2)
    col = lax.rem(me // 2, 2)
    sib = me + 1 - 2 * core
    near = me + 2 - 4 * col
    onward = lax.rem(me + 4 - 8 * col + count, count)
    behind = lax.rem(me - 4 + 8 * col + count, count)
    near_slot = 4 - 4 * col
    far_slot = 4 * col
    sib_slot = 3 - 2 * core
    oth_slot = 1 + 2 * core
    through_slot = 4 - 4 * core

    def partner(level):
        step = 1 << level
        return me + step - 2 * step * lax.rem(me // step, 2)

    def offset(steps):
        return lax.rem(me + steps + count, count)

    def remote(src, dst, send, recv, device):
        return pltpu.make_async_remote_copy(
            src_ref=src,
            dst_ref=dst,
            send_sem=send,
            recv_sem=recv,
            device_id={"space": device},
            device_id_type=MESH,
        )

    barrier = pltpu.get_barrier_semaphore()
    greeted = [offset(steps) for steps in (-1, 1, -2, 2, -4, 4)]
    greeted += [partner(level) for level in range(3, rounds)]
    for device in greeted:
        pl.semaphore_signal(barrier, inc=1, device_id={"space": device}, device_id_type=MESH)

    feat_win[2] = feat_ref[...]
    pos_win[2] = jnp.zeros(pos_win.shape[1:], f32)
    pos_win[2, 0:3] = pos_ref[...]
    table_pad[...] = jnp.zeros(table_pad.shape, f32)
    table_pad[0 : scale_ref.shape[0]] = scale_ref[...]

    pl.semaphore_wait(barrier, len(greeted))

    def cast_start(win, send, recv):
        copies = []
        for j in range(comps):
            copies.append(
                remote(win.at[2, j], win.at[far_slot, j], send.at[0, j], recv.at[far_slot, j], near)
            )
            copies[-1].start()
        for j in range(comps):
            copies.append(
                remote(win.at[2, j], win.at[oth_slot, j], send.at[1, j], recv.at[oth_slot, j], sib)
            )
            copies[-1].start()
        return copies

    def arrived(win, send, recv, slot, j):
        remote(win.at[2, j], win.at[slot, j], send.at[0, j], recv.at[slot, j], near).wait_recv()

    def cast_relay(win, send, recv):
        copies = []
        for j in range(comps):
            arrived(win, send, recv, near_slot, j)
            copies.append(
                remote(
                    win.at[near_slot, j],
                    win.at[far_slot, j],
                    send.at[2, j],
                    recv.at[far_slot, j],
                    onward,
                )
            )
            copies[-1].start()
        return copies

    def cast_finish(win, send, recv):
        copies = []
        for j in range(comps):
            arrived(win, send, recv, far_slot, j)
            copies.append(
                remote(
                    win.at[through_slot, j],
                    win.at[sib_slot, j],
                    send.at[3, j],
                    recv.at[sib_slot, j],
                    sib,
                )
            )
            copies[-1].start()
        for j in range(comps):
            arrived(win, send, recv, sib_slot, j)
            arrived(win, send, recv, oth_slot, j)
        return copies

    pending = []
    pos_copies = []
    for w in (0, 1, 3, 4):
        copy = remote(
            pos_win.at[2],
            pos_win.at[4 - w],
            pos_send.at[w],
            pos_recv.at[4 - w],
            offset(w - 2),
        )
        copy.start()
        pos_copies.append(copy)
    pending += cast_start(feat_win, feat_send, feat_recv)

    species_cols = lax.broadcasted_iota(jnp.int32, (atoms, atoms), 0) == species_ref[...]
    one_hot = jnp.transpose(species_cols.astype(f32))
    scale_buf[...] = jnp.dot(
        one_hot, table_pad[...], precision=highest, preferred_element_type=f32
    )

    def window_of(block):
        return jnp.clip(lax.rem(block - me + REACH + 2 * count, count), 0, 2 * REACH)

    recv_idx = [window_of(table_ref[0, s]) for s in range(slots)]
    send_idx = [window_of(table_ref[1, s]) for s in range(slots)]
    live = [jnp.where(s < live_ref[0], 1.0, 0.0).astype(f32) for s in range(slots)]

    for copy in pos_copies:
        copy.wait_send()
    for w in (0, 1, 3, 4):
        remote(
            pos_win.at[2], pos_win.at[w], pos_send.at[w], pos_recv.at[w], offset(w - 2)
        ).wait_recv()

    pending += cast_relay(feat_win, feat_send, feat_recv)

    for s in range(slots):
        columns = jnp.transpose(pos_win[recv_idx[s]])
        rows = pos_win[send_idx[s]]
        offsets = [rows[x : x + 1, :] - columns[:, x : x + 1] for x in range(3)]
        dist = jnp.sqrt(
            offsets[0] * offsets[0] + offsets[1] * offsets[1] + offsets[2] * offsets[2] + soft_core
        )
        inverse = 1.0 / dist
        dist_buf[s] = dist
        for x in range(3):
            unit_buf[s, x] = offsets[x] * inverse

        def build(k, carry, s=s):
            scaled = dist_buf[s] - (centre_start + k.astype(f32))
            masked = jnp.exp(-scaled * scaled) * mask_ref[s].astype(f32)
            masked_buf[s, k] = masked
            lefts[s, k, 0] = masked.astype(bf16)
            for x in range(3):
                lefts[s, k, 1 + x] = (masked * unit_buf[s, x]).astype(bf16)
            return carry

        lax.fori_loop(0, basis, build, 0)

    pending += cast_finish(feat_win, feat_send, feat_recv)

    for s in range(slots):
        sent = feat_win[send_idx[s]]
        wide = jnp.concatenate([sent[j] for j in range(4)], axis=1)
        tall = sent[1:].reshape(3 * atoms, channels)

        def messages(k, carry, s=s, wide=wide, tall=tall, sent=sent):
            left = lefts[s, k]
            weight = [radial_ref[path, pl.ds(k, 1), :] for path in range(4)]
            plain = dot(left[0], wide)
            along = dot(left[1:].reshape(3 * atoms, atoms), sent[0])
            inner = dot(jnp.concatenate([left[1], left[2], left[3]], axis=1), tall)
            acc[s, 0] += weight[0] * plain[:, :channels] + weight[1] * inner
            for x in range(3):
                acc[s, 1 + x] += (
                    weight[2] * along[x * atoms : (x + 1) * atoms]
                    + weight[3] * plain[:, (1 + x) * channels : (2 + x) * channels]
                )
            return carry

        acc[s] = jnp.zeros(acc.shape[1:], f32)
        lax.fori_loop(0, basis, messages, 0)

    share = [
        [jnp.where(recv_idx[s] == w, live[s], 0.0) for s in range(slots)] for w in range(WINDOW)
    ]
    for j in range(comps):
        for w in range(WINDOW):
            total = share[w][0] * acc[0, j]
            for s in range(1, slots):
                total = total + share[w][s] * acc[s, j]
            partial[w, j] = total
        sib_out[j, 0] = partial[oth_slot, j]
        sib_out[j, 1] = partial[sib_slot, j]
        copy = remote(sib_out.at[j], sib_in.at[j], msg_send.at[0, j], msg_recv.at[0, j], sib)
        copy.start()
        pending.append(copy)

    for j in range(comps):
        remote(sib_out.at[j], sib_in.at[j], msg_send.at[0, j], msg_recv.at[0, j], sib).wait_recv()
        partial[through_slot, j] += sib_in[j, 0]
        far_out[j] = partial[far_slot, j]
        copy = remote(far_out.at[j], far_in.at[j], msg_send.at[1, j], msg_recv.at[1, j], behind)
        copy.start()
        pending.append(copy)
    for j in range(comps):
        remote(far_out.at[j], far_in.at[j], msg_send.at[1, j], msg_recv.at[1, j], behind).wait_recv()
        near_out[j] = partial[near_slot, j] + far_in[j]
        copy = remote(near_out.at[j], near_in.at[j], msg_send.at[2, j], msg_recv.at[2, j], near)
        copy.start()
        pending.append(copy)
    gathered = []
    for j in range(comps):
        remote(near_out.at[j], near_in.at[j], msg_send.at[2, j], msg_recv.at[2, j], near).wait_recv()
        gathered.append(partial[2, j] + sib_in[j, 1] + near_in[j])

    scale = scale_buf[...]
    squares = gathered[1] * gathered[1] + gathered[2] * gathered[2] + gathered[3] * gathered[3]
    invariant = (scale * (gathered[0] + squares)).astype(bf16)
    low_rank = dot(invariant, down_ref[...]).astype(bf16)
    hidden = dot(invariant, mix_ref[...]) + dot(low_rank, up_ref[...])
    sigma = jax.nn.sigmoid(hidden)
    weight_cols = jnp.transpose(jnp.broadcast_to(weight_ref[...], (atoms, atoms)))
    if channels != atoms:
        weight_cols = jnp.broadcast_to(weight_cols[:, :1], (atoms, channels))
    slope = sigma * (1.0 + hidden * (1.0 - sigma))
    grad_pre = (weight_cols * readout_ref[...] * slope).astype(bf16)
    grad_low = dot_trailing(grad_pre, up_ref[...]).astype(bf16)
    grad_inv = dot_trailing(grad_pre, mix_ref[...]) + dot_trailing(grad_low, down_ref[...])
    seed = scale * grad_inv
    cot_win[2, 0] = seed.astype(bf16)
    for x in range(3):
        cot_win[2, 1 + x] = (2.0 * seed * gathered[1 + x]).astype(bf16)
    pending += cast_start(cot_win, cot_send, cot_recv)

    rank = up_ref.shape[0]
    ring_out[0, 0:rank] = dot(jnp.transpose(grad_low.astype(f32)).astype(bf16), invariant)
    ring_out[0, rank:] = dot(jnp.transpose(low_rank.astype(f32)).astype(bf16), grad_pre)
    energy_ref[...] = jnp.sum(
        jnp.transpose(hidden * sigma * readout_ref[...]), axis=0, keepdims=True
    )

    def ring_copy(level):
        return remote(
            ring_out.at[level],
            ring_in.at[level],
            ring_send.at[level],
            ring_recv.at[level],
            partner(level),
        )

    def ring_start(level):
        copy = ring_copy(level)
        copy.start()
        pending.append(copy)

    def ring_finish(level):
        ring_copy(level).wait_recv()
        ring_out[level + 1] = ring_out[level] + ring_in[level]

    ring_start(0)
    pending += cast_relay(cot_win, cot_send, cot_recv)
    ring_finish(0)
    ring_start(1)
    pending += cast_finish(cot_win, cot_send, cot_recv)

    lanes = lax.broadcasted_iota(jnp.int32, (atoms, atoms), 1)
    row_ids = lax.broadcasted_iota(jnp.int32, (8, atoms), 0)
    recv_grads, send_grads = [], []
    for s in range(slots):
        sent = feat_win[send_idx[s]]
        wide = jnp.concatenate([sent[j] for j in range(4)], axis=1)
        pairs = [jnp.concatenate([sent[0], sent[1 + x]], axis=1) for x in range(3)]

        def gradients(k, carry, s=s, wide=wide, pairs=pairs):
            weight = [radial_ref[path, pl.ds(k, 1), :] for path in range(4)]
            cot = [cot_win[recv_idx[s], j].astype(f32) for j in range(4)]
            wall = jnp.concatenate(
                [(weight[0] * cot[0]).astype(bf16)]
                + [(weight[3] * cot[1 + x]).astype(bf16) for x in range(3)],
                axis=1,
            )
            inner = (weight[1] * cot[0]).astype(bf16)
            total = dot_trailing(wall, wide)
            masked = masked_buf[s, k]
            for x in range(3):
                along = (weight[2] * cot[1 + x]).astype(bf16)
                grad_dir = dot_trailing(jnp.concatenate([along, inner], axis=1), pairs[x])
                total = total + grad_dir * unit_buf[s, x]
                grad_unit[x] += masked * grad_dir
            scaled = dist_buf[s] - (centre_start + k.astype(f32))
            grad_dist[...] += total * masked * (-2.0 * scaled)
            return carry

        grad_dist[...] = jnp.zeros(grad_dist.shape, f32)
        grad_unit[...] = jnp.zeros(grad_unit.shape, f32)
        lax.fori_loop(0, basis, gradients, 0)
        units = [unit_buf[s, x] for x in range(3)]
        dirs = [grad_unit[x] for x in range(3)]
        radial_part = dirs[0] * units[0] + dirs[1] * units[1] + dirs[2] * units[2]
        inverse = 1.0 / dist_buf[s]
        columns = jnp.zeros((atoms, atoms), f32)
        send_rows = jnp.zeros((8, atoms), f32)
        for x in range(3):
            grad = grad_dist[...] * units[x] + (dirs[x] - units[x] * radial_part) * inverse
            columns = jnp.where(lanes == x, jnp.sum(grad, axis=1, keepdims=True), columns)
            send_rows = jnp.where(row_ids == x, jnp.sum(grad, axis=0, keepdims=True), send_rows)
        recv_grads.append(-jnp.transpose(columns)[0:8])
        send_grads.append(send_rows)
        if s + 1 < min(rounds, slots):
            ring_finish(s + 1)
            ring_start(s + 2)

    for w in range(WINDOW):
        total = jnp.zeros((8, atoms), f32)
        for s in range(slots):
            total = total + share[w][s] * recv_grads[s]
            total = total + jnp.where(send_idx[s] == w, live[s], 0.0) * send_grads[s]
        grad_out[w] = total
    for w in (0, 1, 3, 4):
        copy = remote(
            grad_out.at[w],
            grad_in.at[4 - w],
            grad_send.at[w],
            grad_recv.at[4 - w],
            offset(w - 2),
        )
        copy.start()
        pending.append(copy)
    for level in range(slots, rounds):
        ring_finish(level)
        if level + 1 < rounds:
            ring_start(level + 1)
    coord = grad_out[2]
    for w in (0, 1, 3, 4):
        remote(
            grad_out.at[w], grad_in.at[w], grad_send.at[w], grad_recv.at[w], offset(w - 2)
        ).wait_recv()
        coord = coord + grad_in[w]
    coord_ref[...] = coord[0:3]
    down_grad_ref[...] = jnp.transpose(ring_out[rounds, 0:rank])
    up_grad_ref[...] = ring_out[rounds, rank:]
    for copy in pending:
        copy.wait_send()


def body(
    features,
    positions,
    species,
    block_pair_table,
    device_pair_count,
    edge_tile_masks,
    radial,
    element_scale_table,
    linear_mixing_weight,
    down_adapter_weight,
    up_adapter_weight,
    readout_weight,
    atom_energy_weight,
):
    count = lax.axis_size("space")
    rounds = count.bit_length() - 1
    assert count == 1 << rounds and rounds >= 3
    atoms, comps, channels = features.shape
    slots = edge_tile_masks.shape[0]
    basis = radial.shape[1]
    rank = up_adapter_weight.shape[0]
    vmem = pl.BlockSpec(memory_space=pltpu.VMEM)
    smem = pl.BlockSpec(memory_space=pltpu.SMEM)
    dma = pltpu.SemaphoreType.DMA
    block = (comps, atoms, channels)
    energies, coordinate_gradient, down_gradient, up_gradient = pl.pallas_call(
        functools.partial(kernel, count, rounds),
        out_shape=(
            jax.ShapeDtypeStruct((1, atoms), f32),
            jax.ShapeDtypeStruct((3, atoms), f32),
            jax.ShapeDtypeStruct((channels, rank), f32),
            jax.ShapeDtypeStruct((rank, channels), f32),
        ),
        in_specs=[smem, smem] + [vmem] * 11,
        out_specs=(vmem,) * 4,
        scratch_shapes=[
            pltpu.VMEM((WINDOW,) + block, bf16),
            pltpu.VMEM((WINDOW,) + block, bf16),
            pltpu.VMEM((WINDOW, 8, atoms), f32),
            pltpu.VMEM((WINDOW,) + block, f32),
            pltpu.VMEM((comps, 2, atoms, channels), f32),
            pltpu.VMEM((comps, 2, atoms, channels), f32),
            pltpu.VMEM(block, f32),
            pltpu.VMEM(block, f32),
            pltpu.VMEM(block, f32),
            pltpu.VMEM(block, f32),
            pltpu.VMEM((slots, basis, 4, atoms, atoms), bf16),
            pltpu.VMEM((slots, basis, atoms, atoms), f32),
            pltpu.VMEM((slots, atoms, atoms), f32),
            pltpu.VMEM((slots, 3, atoms, atoms), f32),
            pltpu.VMEM((slots,) + block, f32),
            pltpu.VMEM((atoms, atoms), f32),
            pltpu.VMEM((3, atoms, atoms), f32),
            pltpu.VMEM((atoms, channels), f32),
            pltpu.VMEM((128, channels), f32),
            pltpu.VMEM((WINDOW, 8, atoms), f32),
            pltpu.VMEM((WINDOW, 8, atoms), f32),
            pltpu.VMEM((rounds + 1, 2 * rank, channels), f32),
            pltpu.VMEM((rounds, 2 * rank, channels), f32),
            dma((4, comps)),
            dma((WINDOW, comps)),
            dma((4, comps)),
            dma((WINDOW, comps)),
            dma((WINDOW,)),
            dma((WINDOW,)),
            dma((3, comps)),
            dma((3, comps)),
            dma((WINDOW,)),
            dma((WINDOW,)),
            dma((rounds,)),
            dma((rounds,)),
        ],
        compiler_params=pltpu.CompilerParams(
            collective_id=0, has_side_effects=True, vmem_limit_bytes=40 * 1024 * 1024
        ),
    )(
        block_pair_table,
        device_pair_count,
        jnp.transpose(features, (1, 0, 2)),
        positions,
        species.reshape(1, atoms),
        edge_tile_masks,
        radial,
        element_scale_table,
        linear_mixing_weight,
        down_adapter_weight,
        up_adapter_weight,
        readout_weight.reshape(1, channels),
        atom_energy_weight.reshape(1, atoms),
    )
    return (energies.reshape(atoms), coordinate_gradient, down_gradient, up_gradient)


def solution(mesh):
    placed = (
        P(("groups", "space"), None, None),
        P(None, ("groups", "space")),
        P(("groups", "space")),
        P(None, ("groups", "space")),
        P(("groups", "space")),
        P(("groups", "space"), None, None),
        P(),
        P(),
        P(),
        P(),
        P(),
        P(),
        P(("groups", "space")),
    )
    return jax.shard_map(
        body,
        mesh=mesh,
        in_specs=placed,
        out_specs=(
            P(("groups", "space")),
            P(None, ("groups", "space")),
            P("groups", None),
            P("groups", None),
        ),
        check_vma=False,
    )
```

```python
import functools

import jax
import jax.numpy as jnp
from jax import lax
from jax.experimental import pallas as pl
from jax.experimental.pallas import tpu as pltpu
from jax.sharding import PartitionSpec as P

REACH = 2
WINDOW = 2 * REACH + 1

soft_core = 0.25
centre_start = 1.0
highest = lax.Precision.HIGHEST
MESH = pl.DeviceIdType.MESH
f32 = jnp.float32
bf16 = jnp.bfloat16


def dot(left, right):
    return jnp.dot(left, right, preferred_element_type=f32)


def dot_trailing(left, right):
    return lax.dot_general(left, right, (((1,), (1,)), ((), ())), preferred_element_type=f32)


def kernel(
    count,
    rounds,
    table_ref,
    live_ref,
    feat_ref,
    pos_ref,
    species_ref,
    mask_ref,
    radial_ref,
    scale_ref,
    mix_ref,
    down_ref,
    up_ref,
    readout_ref,
    weight_ref,
    energy_ref,
    coord_ref,
    adapter_ref,
    feat_win,
    agg_win,
    pos_win,
    partial,
    sib_in,
    far_in,
    near_in,
    lefts,
    masked_buf,
    dist_buf,
    unit_buf,
    scale_buf,
    table_pad,
    grad_out,
    grad_in,
    ring_out,
    ring_in,
    feat_send,
    feat_recv,
    cot_send,
    cot_recv,
    pos_send,
    pos_recv,
    msg_send,
    msg_recv,
    grad_send,
    grad_recv,
    ring_send,
    ring_recv,
):
    comps, atoms, channels = feat_ref.shape
    slots = mask_ref.shape[0]
    basis = radial_ref.shape[1]
    me = lax.axis_index("space")
    core = lax.rem(me, 2)
    col = lax.rem(me // 2, 2)
    sib = me + 1 - 2 * core
    near = me + 2 - 4 * col
    onward = lax.rem(me + 4 - 8 * col + count, count)
    behind = lax.rem(me - 4 + 8 * col + count, count)
    near_slot = 4 - 4 * col
    far_slot = 4 * col
    sib_slot = 3 - 2 * core
    oth_slot = 1 + 2 * core
    through_slot = 4 - 4 * core

    def partner(level):
        step = 1 << level
        return me + step - 2 * step * lax.rem(me // step, 2)

    def offset(steps):
        return lax.rem(me + steps + count, count)

    def remote(src, dst, send, recv, device):
        return pltpu.make_async_remote_copy(
            src_ref=src,
            dst_ref=dst,
            send_sem=send,
            recv_sem=recv,
            device_id={"space": device},
            device_id_type=MESH,
        )

    barrier = pltpu.get_barrier_semaphore()
    greeted = [offset(steps) for steps in (-1, 1, -2, 2, -4, 4)]
    greeted += [partner(level) for level in range(3, rounds)]
    for device in greeted:
        pl.semaphore_signal(barrier, inc=1, device_id={"space": device}, device_id_type=MESH)

    feat_win[2] = feat_ref[...]
    pos_win[2] = jnp.zeros(pos_win.shape[1:], f32)
    pos_win[2, 0:3] = pos_ref[...]
    table_pad[...] = jnp.zeros(table_pad.shape, f32)
    table_pad[0 : scale_ref.shape[0]] = scale_ref[...]

    pl.semaphore_wait(barrier, len(greeted))

    def cast_start(win, send, recv, parts):
        copies = []
        for target, slot, kind in ((near, far_slot, 0), (sib, oth_slot, 1)):
            for j in parts:
                copies.append(
                    remote(win.at[2, j], win.at[slot, j], send.at[kind, j], recv.at[slot, j], target)
                )
                copies[-1].start()
        return copies

    def arrived(win, send, recv, slot, j):
        remote(win.at[2, j], win.at[slot, j], send.at[0, j], recv.at[slot, j], near).wait_recv()

    def cast_relay(win, send, recv, parts):
        copies = []
        for j in parts:
            arrived(win, send, recv, near_slot, j)
            copies.append(
                remote(
                    win.at[near_slot, j],
                    win.at[far_slot, j],
                    send.at[2, j],
                    recv.at[far_slot, j],
                    onward,
                )
            )
            copies[-1].start()
        return copies

    def cast_forward(win, send, recv, parts):
        copies = []
        for j in parts:
            arrived(win, send, recv, far_slot, j)
            copies.append(
                remote(
                    win.at[through_slot, j],
                    win.at[sib_slot, j],
                    send.at[3, j],
                    recv.at[sib_slot, j],
                    sib,
                )
            )
            copies[-1].start()
        return copies

    def cast_finish(win, send, recv, parts):
        for j in parts:
            arrived(win, send, recv, sib_slot, j)
            arrived(win, send, recv, oth_slot, j)

    order = (1, 2, 3, 0)
    pending = []
    pos_copies = []
    for w in (0, 1, 3, 4):
        copy = remote(
            pos_win.at[2],
            pos_win.at[4 - w],
            pos_send.at[w],
            pos_recv.at[4 - w],
            offset(w - 2),
        )
        copy.start()
        pos_copies.append(copy)
    pending += cast_start(feat_win, feat_send, feat_recv, range(comps))

    species_cols = lax.broadcasted_iota(jnp.int32, (atoms, atoms), 0) == species_ref[...]
    one_hot = jnp.transpose(species_cols.astype(f32))
    scale_buf[...] = jnp.dot(
        one_hot, table_pad[...], precision=highest, preferred_element_type=f32
    )

    def window_of(block):
        return jnp.clip(lax.rem(block - me + REACH + 2 * count, count), 0, 2 * REACH)

    recv_idx = [window_of(table_ref[0, s]) for s in range(slots)]
    send_idx = [window_of(table_ref[1, s]) for s in range(slots)]
    live = [jnp.where(s < live_ref[0], 1.0, 0.0).astype(f32) for s in range(slots)]

    for copy in pos_copies:
        copy.wait_send()
    for w in (0, 1, 3, 4):
        remote(
            pos_win.at[2], pos_win.at[w], pos_send.at[w], pos_recv.at[w], offset(w - 2)
        ).wait_recv()

    pending += cast_relay(feat_win, feat_send, feat_recv, range(comps))

    for s in range(slots):
        columns = jnp.transpose(pos_win[recv_idx[s]])
        rows = pos_win[send_idx[s]]
        offsets = [rows[x : x + 1, :] - columns[:, x : x + 1] for x in range(3)]
        dist = jnp.sqrt(
            offsets[0] * offsets[0] + offsets[1] * offsets[1] + offsets[2] * offsets[2] + soft_core
        )
        inverse = 1.0 / dist
        dist_buf[s] = dist
        for x in range(3):
            unit_buf[s, x] = offsets[x] * inverse

        def build(k, carry, s=s):
            scaled = dist_buf[s] - (centre_start + k.astype(f32))
            masked = jnp.exp(-scaled * scaled) * mask_ref[s].astype(f32)
            masked_buf[s, k] = masked
            lefts[s, 0, k] = masked.astype(bf16)
            for x in range(3):
                lefts[s, 1 + x, k] = (masked * unit_buf[s, x]).astype(bf16)
            return carry

        lax.fori_loop(0, basis, build, 0)

    pending += cast_forward(feat_win, feat_send, feat_recv, range(comps))
    cast_finish(feat_win, feat_send, feat_recv, range(comps))

    share = [
        [jnp.where(recv_idx[s] == w, live[s], 0.0) for s in range(slots)] for w in range(WINDOW)
    ]

    def weighted(product, path):
        total = radial_ref[path, 0:1, :] * product[0:atoms]
        for k in range(1, basis):
            total = total + radial_ref[path, k : k + 1, :] * product[k * atoms : (k + 1) * atoms]
        return total

    def component(j):
        terms = []
        for s in range(slots):
            plain = lefts[s, 0].reshape(basis * atoms, atoms)
            straight = dot(plain, feat_win[send_idx[s], j])
            if j == 0:
                turned = [lefts[s, 1 + x].reshape(basis * atoms, atoms) for x in range(3)]
                tall = feat_win[send_idx[s]][1:].reshape(3 * atoms, channels)
                crossed = dot(jnp.concatenate(turned, axis=1), tall)
                terms.append(weighted(straight, 0) + weighted(crossed, 1))
            else:
                turned = lefts[s, j].reshape(basis * atoms, atoms)
                crossed = dot(turned, feat_win[send_idx[s], 0])
                terms.append(weighted(crossed, 2) + weighted(straight, 3))
        for w in range(WINDOW):
            total = share[w][0] * terms[0]
            for s in range(1, slots):
                total = total + share[w][s] * terms[s]
            partial[w, j] = total

    def message_copy(hop, j):
        src, dst, device = (
            (partial.at[oth_slot, j], sib_in.at[0, j], sib),
            (partial.at[sib_slot, j], sib_in.at[1, j], sib),
            (partial.at[far_slot, j], far_in.at[j], behind),
            (partial.at[near_slot, j], near_in.at[j], near),
        )[hop]
        return remote(src, dst, msg_send.at[hop, j], msg_recv.at[hop, j], device)

    def message_start(hop, j):
        copy = message_copy(hop, j)
        copy.start()
        pending.append(copy)

    def to_sib(j):
        component(j)
        message_start(0, j)
        message_start(1, j)

    def to_far(j):
        message_copy(0, j).wait_recv()
        partial[through_slot, j] += sib_in[0, j]
        message_start(2, j)

    def to_near(j):
        message_copy(2, j).wait_recv()
        partial[near_slot, j] += far_in[j]
        message_start(3, j)

    def gather(j):
        message_copy(1, j).wait_recv()
        message_copy(3, j).wait_recv()
        return partial[2, j] + sib_in[1, j] + near_in[j]

    to_sib(1)
    to_sib(2)
    to_far(1)
    to_sib(3)
    to_far(2)
    to_sib(0)
    to_near(1)
    to_far(3)
    to_far(0)
    to_near(2)
    to_near(3)
    for j in (1, 2, 3):
        agg_win[2, j] = gather(j)
        pending += cast_start(agg_win, cot_send, cot_recv, (j,))
        if j == 1:
            to_near(0)
    gathered = [gather(0)] + [agg_win[2, j] for j in (1, 2, 3)]

    scale = scale_buf[...]
    squares = gathered[1] * gathered[1] + gathered[2] * gathered[2] + gathered[3] * gathered[3]
    invariant = (scale * (gathered[0] + squares)).astype(bf16)
    low_rank = dot(invariant, down_ref[...]).astype(bf16)
    hidden = dot(invariant, mix_ref[...]) + dot(low_rank, up_ref[...])
    sigma = jax.nn.sigmoid(hidden)
    weight_cols = jnp.transpose(jnp.broadcast_to(weight_ref[...], (atoms, atoms)))
    if channels != atoms:
        weight_cols = jnp.broadcast_to(weight_cols[:, :1], (atoms, channels))
    slope = sigma * (1.0 + hidden * (1.0 - sigma))
    grad_pre = (weight_cols * readout_ref[...] * slope).astype(bf16)
    grad_low = dot_trailing(grad_pre, up_ref[...]).astype(bf16)
    grad_inv = dot_trailing(grad_pre, mix_ref[...]) + dot_trailing(grad_low, down_ref[...])
    seed = scale * grad_inv
    agg_win[2, 0] = seed
    pending += cast_start(agg_win, cot_send, cot_recv, (0,))

    rank = up_ref.shape[0]
    ring_out[0, 0:rank] = dot(jnp.transpose(grad_low.astype(f32)).astype(bf16), invariant)
    ring_out[0, rank:] = dot(jnp.transpose(low_rank.astype(f32)).astype(bf16), grad_pre)
    energy_ref[...] = jnp.sum(
        jnp.transpose(hidden * sigma * readout_ref[...]), axis=0, keepdims=True
    )

    def ring_copy(level):
        return remote(
            ring_out.at[level],
            ring_in.at[level],
            ring_send.at[level],
            ring_recv.at[level],
            partner(level),
        )

    def ring_start(level):
        copy = ring_copy(level)
        copy.start()
        pending.append(copy)

    def ring_finish(level):
        ring_copy(level).wait_recv()
        ring_out[level + 1] = ring_out[level] + ring_in[level]

    ring_start(0)
    pending += cast_relay(agg_win, cot_send, cot_recv, order)
    ring_finish(0)
    ring_start(1)
    pending += cast_forward(agg_win, cot_send, cot_recv, order)
    cast_finish(agg_win, cot_send, cot_recv, order)

    lanes = lax.broadcasted_iota(jnp.int32, (atoms, atoms), 1)
    row_ids = lax.broadcasted_iota(jnp.int32, (8, atoms), 0)
    recv_grads, send_grads = [], []
    for s in range(slots):
        sent = feat_win[send_idx[s]]
        wide = jnp.concatenate([sent[j] for j in range(4)], axis=1)
        pairs = [jnp.concatenate([sent[0], sent[1 + x]], axis=1) for x in range(3)]

        cot = [agg_win[recv_idx[s], 0]]
        for x in range(3):
            cot.append(2.0 * cot[0] * agg_win[recv_idx[s], 1 + x])
        gap = dist_buf[s]
        units = [unit_buf[s, x] for x in range(3)]
        grad_dist = jnp.zeros((atoms, atoms), f32)
        dirs = [jnp.zeros((atoms, atoms), f32) for x in range(3)]
        for k in range(basis):
            weight = [radial_ref[path, k : k + 1, :] for path in range(4)]
            wall = jnp.concatenate(
                [(weight[0] * cot[0]).astype(bf16)]
                + [(weight[3] * cot[1 + x]).astype(bf16) for x in range(3)],
                axis=1,
            )
            inner = (weight[1] * cot[0]).astype(bf16)
            total = dot_trailing(wall, wide)
            masked = masked_buf[s, k]
            for x in range(3):
                along = (weight[2] * cot[1 + x]).astype(bf16)
                grad_dir = dot_trailing(jnp.concatenate([along, inner], axis=1), pairs[x])
                total = total + grad_dir * units[x]
                dirs[x] = dirs[x] + masked * grad_dir
            grad_dist = grad_dist + total * masked * (-2.0 * (gap - (centre_start + k)))
        radial_part = dirs[0] * units[0] + dirs[1] * units[1] + dirs[2] * units[2]
        inverse = 1.0 / gap
        columns = jnp.zeros((atoms, atoms), f32)
        send_rows = jnp.zeros((8, atoms), f32)
        for x in range(3):
            grad = grad_dist * units[x] + (dirs[x] - units[x] * radial_part) * inverse
            columns = jnp.where(lanes == x, jnp.sum(grad, axis=1, keepdims=True), columns)
            send_rows = jnp.where(row_ids == x, jnp.sum(grad, axis=0, keepdims=True), send_rows)
        recv_grads.append(-jnp.transpose(columns)[0:8])
        send_grads.append(send_rows)
        if s + 1 < min(rounds, slots):
            ring_finish(s + 1)
            ring_start(s + 2)

    for w in range(WINDOW):
        total = jnp.zeros((8, atoms), f32)
        for s in range(slots):
            total = total + share[w][s] * recv_grads[s]
            total = total + jnp.where(send_idx[s] == w, live[s], 0.0) * send_grads[s]
        grad_out[w] = total
    for w in (0, 1, 3, 4):
        copy = remote(
            grad_out.at[w],
            grad_in.at[4 - w],
            grad_send.at[w],
            grad_recv.at[4 - w],
            offset(w - 2),
        )
        copy.start()
        pending.append(copy)
    for level in range(slots, rounds):
        ring_finish(level)
        if level + 1 < rounds:
            ring_start(level + 1)
    coord = grad_out[2]
    for w in (0, 1, 3, 4):
        remote(
            grad_out.at[w], grad_in.at[w], grad_send.at[w], grad_recv.at[w], offset(w - 2)
        ).wait_recv()
        coord = coord + grad_in[w]
    coord_ref[...] = coord
    adapter_ref[...] = ring_out[rounds]
    for copy in pending:
        copy.wait_send()


def finish(energy_in, coord_in, adapter_in, energy_ref, coord_ref, down_ref, up_ref):
    rank = up_ref.shape[0]
    energy_ref[...] = energy_in[...]
    coord_ref[...] = coord_in[0:3]
    down_ref[...] = jnp.transpose(adapter_in[0:rank])
    up_ref[...] = adapter_in[rank:]


def body(
    features,
    positions,
    species,
    block_pair_table,
    device_pair_count,
    edge_tile_masks,
    radial,
    element_scale_table,
    linear_mixing_weight,
    down_adapter_weight,
    up_adapter_weight,
    readout_weight,
    atom_energy_weight,
):
    count = lax.axis_size("space")
    rounds = count.bit_length() - 1
    assert count == 1 << rounds and rounds >= 3
    atoms, comps, channels = features.shape
    slots = edge_tile_masks.shape[0]
    basis = radial.shape[1]
    rank = up_adapter_weight.shape[0]
    vmem = pl.BlockSpec(memory_space=pltpu.VMEM)
    smem = pl.BlockSpec(memory_space=pltpu.SMEM)
    dma = pltpu.SemaphoreType.DMA
    block = (comps, atoms, channels)
    energy_row, coord_rows, adapter_rows = pl.pallas_call(
        functools.partial(kernel, count, rounds),
        out_shape=(
            jax.ShapeDtypeStruct((1, atoms), f32),
            jax.ShapeDtypeStruct((8, atoms), f32),
            jax.ShapeDtypeStruct((2 * rank, channels), f32),
        ),
        in_specs=[smem, smem] + [vmem] * 11,
        out_specs=(vmem,) * 3,
        scratch_shapes=[
            pltpu.VMEM((WINDOW,) + block, bf16),
            pltpu.VMEM((WINDOW,) + block, f32),
            pltpu.VMEM((WINDOW, 8, atoms), f32),
            pltpu.VMEM((WINDOW,) + block, f32),
            pltpu.VMEM((2,) + block, f32),
            pltpu.VMEM(block, f32),
            pltpu.VMEM(block, f32),
            pltpu.VMEM((slots, 4, basis, atoms, atoms), bf16),
            pltpu.VMEM((slots, basis, atoms, atoms), f32),
            pltpu.VMEM((slots, atoms, atoms), f32),
            pltpu.VMEM((slots, 3, atoms, atoms), f32),
            pltpu.VMEM((atoms, channels), f32),
            pltpu.VMEM((128, channels), f32),
            pltpu.VMEM((WINDOW, 8, atoms), f32),
            pltpu.VMEM((WINDOW, 8, atoms), f32),
            pltpu.VMEM((rounds + 1, 2 * rank, channels), f32),
            pltpu.VMEM((rounds, 2 * rank, channels), f32),
            dma((4, comps)),
            dma((WINDOW, comps)),
            dma((4, comps)),
            dma((WINDOW, comps)),
            dma((WINDOW,)),
            dma((WINDOW,)),
            dma((4, comps)),
            dma((4, comps)),
            dma((WINDOW,)),
            dma((WINDOW,)),
            dma((rounds,)),
            dma((rounds,)),
        ],
        compiler_params=pltpu.CompilerParams(
            collective_id=0, has_side_effects=True, vmem_limit_bytes=40 * 1024 * 1024
        ),
    )(
        block_pair_table,
        device_pair_count,
        jnp.transpose(features, (1, 0, 2)),
        positions,
        species.reshape(1, atoms),
        edge_tile_masks,
        radial,
        element_scale_table,
        linear_mixing_weight,
        down_adapter_weight,
        up_adapter_weight,
        readout_weight.reshape(1, channels),
        atom_energy_weight.reshape(1, atoms),
    )
    energies, coordinate_gradient, down_gradient, up_gradient = pl.pallas_call(
        finish,
        out_shape=(
            jax.ShapeDtypeStruct((1, atoms), f32),
            jax.ShapeDtypeStruct((3, atoms), f32),
            jax.ShapeDtypeStruct((channels, rank), f32),
            jax.ShapeDtypeStruct((rank, channels), f32),
        ),
    )(energy_row, coord_rows, adapter_rows)
    return (energies.reshape(atoms), coordinate_gradient, down_gradient, up_gradient)


def solution(mesh):
    placed = (
        P(("groups", "space"), None, None),
        P(None, ("groups", "space")),
        P(("groups", "space")),
        P(None, ("groups", "space")),
        P(("groups", "space")),
        P(("groups", "space"), None, None),
        P(),
        P(),
        P(),
        P(),
        P(),
        P(),
        P(("groups", "space")),
    )
    return jax.shard_map(
        body,
        mesh=mesh,
        in_specs=placed,
        out_specs=(
            P(("groups", "space")),
            P(None, ("groups", "space")),
            P("groups", None),
            P("groups", None),
        ),
        check_vma=False,
    )
```

```python
import functools

import jax
import jax.numpy as jnp
from jax import lax
from jax.experimental import pallas as pl
from jax.experimental.pallas import tpu as pltpu
from jax.sharding import PartitionSpec as P

REACH = 2
WINDOW = 2 * REACH + 1

soft_core = 0.25
centre_start = 1.0
highest = lax.Precision.HIGHEST
MESH = pl.DeviceIdType.MESH
FEAT_DIRECT = (0, 1, 2, 3)
MSG_DIRECT = (0,)
COT_DIRECT = (0,)
f32 = jnp.float32
bf16 = jnp.bfloat16


def dot(left, right):
    return jnp.dot(left, right, preferred_element_type=f32)


def dot_trailing(left, right):
    return lax.dot_general(left, right, (((1,), (1,)), ((), ())), preferred_element_type=f32)


def kernel(
    count,
    rounds,
    table_ref,
    live_ref,
    feat_ref,
    pos_ref,
    species_ref,
    mask_ref,
    radial_ref,
    scale_ref,
    mix_ref,
    down_ref,
    up_ref,
    readout_ref,
    weight_ref,
    energy_ref,
    coord_ref,
    adapter_ref,
    feat_0,
    feat_1,
    feat_2,
    feat_3,
    agg_0,
    agg_1,
    agg_2,
    agg_3,
    pos_win,
    partial,
    sib_in,
    far_in,
    near_in,
    lefts,
    masked_buf,
    dist_buf,
    unit_buf,
    scale_buf,
    table_pad,
    grad_out,
    grad_in,
    ring_out,
    ring_in,
    feat_send,
    feat_recv,
    cot_send,
    cot_recv,
    pos_send,
    pos_recv,
    msg_send,
    msg_recv,
    grad_send,
    grad_recv,
    ring_send,
    ring_recv,
):
    comps, atoms, channels = feat_ref.shape
    feat_win = (feat_0, feat_1, feat_2, feat_3)
    agg_win = (agg_0, agg_1, agg_2, agg_3)
    slots = mask_ref.shape[0]
    basis = radial_ref.shape[1]
    me = lax.axis_index("space")
    core = lax.rem(me, 2)
    col = lax.rem(me // 2, 2)
    sib = me + 1 - 2 * core
    near = me + 2 - 4 * col
    far = lax.rem(me - 2 + 4 * col + count, count)
    onward = lax.rem(me + 4 - 8 * col + count, count)
    behind = lax.rem(me - 4 + 8 * col + count, count)
    near_slot = 4 - 4 * col
    far_slot = 4 * col
    sib_slot = 3 - 2 * core
    oth_slot = 1 + 2 * core
    through_slot = 4 - 4 * core

    def partner(level):
        step = 1 << level
        return me + step - 2 * step * lax.rem(me // step, 2)

    def offset(steps):
        return lax.rem(me + steps + count, count)

    def remote(src, dst, send, recv, device):
        return pltpu.make_async_remote_copy(
            src_ref=src,
            dst_ref=dst,
            send_sem=send,
            recv_sem=recv,
            device_id={"space": device},
            device_id_type=MESH,
        )

    barrier = pltpu.get_barrier_semaphore()
    greeted = [offset(steps) for steps in (-1, 1, -2, 2, -4, 4)]
    greeted += [partner(level) for level in range(3, rounds)]
    for device in greeted:
        pl.semaphore_signal(barrier, inc=1, device_id={"space": device}, device_id_type=MESH)

    for j in range(comps):
        feat_win[j][2] = feat_ref[j]
    pos_win[2] = jnp.zeros(pos_win.shape[1:], f32)
    pos_win[2, 0:3] = pos_ref[...]
    table_pad[...] = jnp.zeros(table_pad.shape, f32)
    table_pad[0 : scale_ref.shape[0]] = scale_ref[...]

    pl.semaphore_wait(barrier, len(greeted))

    def cast_copy(win, send, recv, kind, j):
        src, dst, device = (
            (2, far_slot, near),
            (2, oth_slot, sib),
            (near_slot, far_slot, onward),
            (through_slot, sib_slot, sib),
            (2, near_slot, far),
        )[kind]
        return remote(
            win[j].at[src], win[j].at[dst], send.at[kind, j], recv.at[dst, j], device
        )

    def cast_begin(win, send, recv, kind, j):
        copy = cast_copy(win, send, recv, kind, j)
        copy.start()
        pending.append(copy)

    def cast_start(win, send, recv, parts, direct):
        for j in parts:
            cast_begin(win, send, recv, 0, j)
            if j in direct:
                cast_begin(win, send, recv, 4, j)
        for j in parts:
            cast_begin(win, send, recv, 1, j)

    def arrived(win, send, recv, slot, j):
        remote(
            win[j].at[2], win[j].at[slot], send.at[0, j], recv.at[slot, j], near
        ).wait_recv()

    def cast_relay(win, send, recv, parts, direct):
        for j in parts:
            if j not in direct:
                arrived(win, send, recv, near_slot, j)
                cast_begin(win, send, recv, 2, j)

    def cast_forward(win, send, recv, parts, direct):
        for j in parts:
            if j in direct:
                arrived(win, send, recv, near_slot, j)
            arrived(win, send, recv, far_slot, j)
            cast_begin(win, send, recv, 3, j)

    def cast_finish(win, send, recv, parts):
        for j in parts:
            arrived(win, send, recv, sib_slot, j)
            arrived(win, send, recv, oth_slot, j)

    order = (1, 2, 3, 0)
    feat = (feat_win, feat_send, feat_recv)
    agg = (agg_win, cot_send, cot_recv)
    pending = []
    pos_copies = []
    for w in (0, 1, 3, 4):
        copy = remote(
            pos_win.at[2],
            pos_win.at[4 - w],
            pos_send.at[w],
            pos_recv.at[4 - w],
            offset(w - 2),
        )
        copy.start()
        pos_copies.append(copy)
    cast_start(*feat, range(comps), FEAT_DIRECT)

    species_cols = lax.broadcasted_iota(jnp.int32, (atoms, atoms), 0) == species_ref[...]
    one_hot = jnp.transpose(species_cols.astype(f32))
    scale_buf[...] = jnp.dot(
        one_hot, table_pad[...], precision=highest, preferred_element_type=f32
    )

    def window_of(block):
        return jnp.clip(lax.rem(block - me + REACH + 2 * count, count), 0, 2 * REACH)

    recv_idx = [window_of(table_ref[0, s]) for s in range(slots)]
    send_idx = [window_of(table_ref[1, s]) for s in range(slots)]
    live = [jnp.where(s < live_ref[0], 1.0, 0.0).astype(f32) for s in range(slots)]

    for copy in pos_copies:
        copy.wait_send()
    for w in (0, 1, 3, 4):
        remote(
            pos_win.at[2], pos_win.at[w], pos_send.at[w], pos_recv.at[w], offset(w - 2)
        ).wait_recv()

    cast_relay(*feat, range(comps), FEAT_DIRECT)

    for s in range(slots):
        columns = jnp.transpose(pos_win[recv_idx[s]])
        rows = pos_win[send_idx[s]]
        offsets = [rows[x : x + 1, :] - columns[:, x : x + 1] for x in range(3)]
        dist = jnp.sqrt(
            offsets[0] * offsets[0] + offsets[1] * offsets[1] + offsets[2] * offsets[2] + soft_core
        )
        inverse = 1.0 / dist
        dist_buf[s] = dist
        for x in range(3):
            unit_buf[s, x] = offsets[x] * inverse

        def build(k, carry, s=s):
            scaled = dist_buf[s] - (centre_start + k.astype(f32))
            masked = jnp.exp(-scaled * scaled) * mask_ref[s].astype(f32)
            masked_buf[s, k] = masked
            lefts[s, 0, k] = masked.astype(bf16)
            for x in range(3):
                lefts[s, 1 + x, k] = (masked * unit_buf[s, x]).astype(bf16)
            return carry

        lax.fori_loop(0, basis, build, 0)

    cast_forward(*feat, (0, 1), FEAT_DIRECT)
    cast_finish(*feat, (0, 1))

    share = [
        [jnp.where(recv_idx[s] == w, live[s], 0.0) for s in range(slots)] for w in range(WINDOW)
    ]

    def weighted(product, path):
        total = radial_ref[path, 0:1, :] * product[0:atoms]
        for k in range(1, basis):
            total = total + radial_ref[path, k : k + 1, :] * product[k * atoms : (k + 1) * atoms]
        return total

    def component(j):
        terms = []
        for s in range(slots):
            plain = lefts[s, 0].reshape(basis * atoms, atoms)
            straight = dot(plain, feat_win[j][send_idx[s]])
            if j == 0:
                turned = [lefts[s, 1 + x].reshape(basis * atoms, atoms) for x in range(3)]
                tall = jnp.concatenate([feat_win[1 + x][send_idx[s]] for x in range(3)], axis=0)
                crossed = dot(jnp.concatenate(turned, axis=1), tall)
                terms.append(weighted(straight, 0) + weighted(crossed, 1))
            else:
                turned = lefts[s, j].reshape(basis * atoms, atoms)
                crossed = dot(turned, feat_win[0][send_idx[s]])
                terms.append(weighted(crossed, 2) + weighted(straight, 3))
        for w in range(WINDOW):
            total = share[w][0] * terms[0]
            for s in range(1, slots):
                total = total + share[w][s] * terms[s]
            partial[w, j] = total

    def message_copy(hop, j):
        src, dst, device = (
            (partial.at[oth_slot, j], sib_in.at[0, j], sib),
            (partial.at[sib_slot, j], sib_in.at[1, j], sib),
            (partial.at[far_slot, j], far_in.at[j], far if j in MSG_DIRECT else behind),
            (partial.at[near_slot, j], near_in.at[j], near),
        )[hop]
        return remote(src, dst, msg_send.at[hop, j], msg_recv.at[hop, j], device)

    def message_start(hop, j):
        copy = message_copy(hop, j)
        copy.start()
        pending.append(copy)

    def to_sib(j):
        component(j)
        message_start(0, j)
        message_start(1, j)

    def to_far(j):
        message_copy(0, j).wait_recv()
        partial[through_slot, j] += sib_in[0, j]
        message_start(2, j)

    def to_near(j):
        if j not in MSG_DIRECT:
            message_copy(2, j).wait_recv()
            partial[near_slot, j] += far_in[j]
        message_start(3, j)

    def gather(j):
        message_copy(1, j).wait_recv()
        total = partial[2, j] + sib_in[1, j]
        if j in MSG_DIRECT:
            message_copy(2, j).wait_recv()
            total = total + far_in[j]
        message_copy(3, j).wait_recv()
        return total + near_in[j]

    to_sib(1)
    cast_forward(*feat, (2,), FEAT_DIRECT)
    cast_finish(*feat, (2,))
    to_sib(2)
    to_far(1)
    cast_forward(*feat, (3,), FEAT_DIRECT)
    cast_finish(*feat, (3,))
    to_sib(3)
    to_far(2)
    to_sib(0)
    to_near(1)
    to_far(3)
    to_far(0)
    if 0 in MSG_DIRECT:
        to_near(0)
    to_near(2)
    to_near(3)
    if 0 not in MSG_DIRECT:
        to_near(0)
    for j in (1, 2, 3):
        agg_win[j][2] = gather(j)
        cast_start(*agg, (j,), COT_DIRECT)
    cast_relay(*agg, (1, 2), COT_DIRECT)
    gathered = [gather(0)] + [agg_win[j][2] for j in (1, 2, 3)]

    scale = scale_buf[...]
    squares = gathered[1] * gathered[1] + gathered[2] * gathered[2] + gathered[3] * gathered[3]
    invariant = (scale * (gathered[0] + squares)).astype(bf16)
    low_rank = dot(invariant, down_ref[...]).astype(bf16)
    hidden = dot(invariant, mix_ref[...]) + dot(low_rank, up_ref[...])
    sigma = jax.nn.sigmoid(hidden)
    weight_cols = jnp.transpose(jnp.broadcast_to(weight_ref[...], (atoms, atoms)))
    if channels != atoms:
        weight_cols = jnp.broadcast_to(weight_cols[:, :1], (atoms, channels))
    slope = sigma * (1.0 + hidden * (1.0 - sigma))
    grad_pre = (weight_cols * readout_ref[...] * slope).astype(bf16)
    grad_low = dot_trailing(grad_pre, up_ref[...]).astype(bf16)
    grad_inv = dot_trailing(grad_pre, mix_ref[...]) + dot_trailing(grad_low, down_ref[...])
    seed = scale * grad_inv
    agg_win[0][2] = seed
    cast_start(*agg, (0,), COT_DIRECT)
    cast_relay(*agg, (3, 0), COT_DIRECT)

    rank = up_ref.shape[0]
    ring_out[0, 0:rank] = dot(jnp.transpose(grad_low.astype(f32)).astype(bf16), invariant)
    ring_out[0, rank:] = dot(jnp.transpose(low_rank.astype(f32)).astype(bf16), grad_pre)
    energy_ref[...] = jnp.sum(
        jnp.transpose(hidden * sigma * readout_ref[...]), axis=0, keepdims=True
    )

    def ring_copy(level):
        return remote(
            ring_out.at[level],
            ring_in.at[level],
            ring_send.at[level],
            ring_recv.at[level],
            partner(level),
        )

    def ring_start(level):
        copy = ring_copy(level)
        copy.start()
        pending.append(copy)

    def ring_finish(level):
        ring_copy(level).wait_recv()
        ring_out[level + 1] = ring_out[level] + ring_in[level]

    ring_start(0)
    ring_finish(0)
    ring_start(1)
    cast_forward(*agg, order, COT_DIRECT)
    cast_finish(*agg, order)

    lanes = lax.broadcasted_iota(jnp.int32, (atoms, atoms), 1)
    row_ids = lax.broadcasted_iota(jnp.int32, (8, atoms), 0)
    recv_grads, send_grads = [], []
    for s in range(slots):
        sent = [feat_win[j][send_idx[s]] for j in range(4)]
        wide = jnp.concatenate(sent, axis=1)
        pairs = [jnp.concatenate([sent[0], sent[1 + x]], axis=1) for x in range(3)]

        cot = [agg_win[0][recv_idx[s]]]
        for x in range(3):
            cot.append(2.0 * cot[0] * agg_win[1 + x][recv_idx[s]])
        gap = dist_buf[s]
        units = [unit_buf[s, x] for x in range(3)]
        grad_dist = jnp.zeros((atoms, atoms), f32)
        dirs = [jnp.zeros((atoms, atoms), f32) for x in range(3)]
        for k in range(basis):
            weight = [radial_ref[path, k : k + 1, :] for path in range(4)]
            wall = jnp.concatenate(
                [(weight[0] * cot[0]).astype(bf16)]
                + [(weight[3] * cot[1 + x]).astype(bf16) for x in range(3)],
                axis=1,
            )
            inner = (weight[1] * cot[0]).astype(bf16)
            total = dot_trailing(wall, wide)
            masked = masked_buf[s, k]
            for x in range(3):
                along = (weight[2] * cot[1 + x]).astype(bf16)
                grad_dir = dot_trailing(jnp.concatenate([along, inner], axis=1), pairs[x])
                total = total + grad_dir * units[x]
                dirs[x] = dirs[x] + masked * grad_dir
            grad_dist = grad_dist + total * masked * (-2.0 * (gap - (centre_start + k)))
        radial_part = dirs[0] * units[0] + dirs[1] * units[1] + dirs[2] * units[2]
        inverse = 1.0 / gap
        columns = jnp.zeros((atoms, atoms), f32)
        send_rows = jnp.zeros((8, atoms), f32)
        for x in range(3):
            grad = grad_dist * units[x] + (dirs[x] - units[x] * radial_part) * inverse
            columns = jnp.where(lanes == x, jnp.sum(grad, axis=1, keepdims=True), columns)
            send_rows = jnp.where(row_ids == x, jnp.sum(grad, axis=0, keepdims=True), send_rows)
        recv_grads.append(-jnp.transpose(columns)[0:8])
        send_grads.append(send_rows)
        if s + 1 < min(rounds, slots):
            ring_finish(s + 1)
            ring_start(s + 2)

    for w in range(WINDOW):
        total = jnp.zeros((8, atoms), f32)
        for s in range(slots):
            total = total + share[w][s] * recv_grads[s]
            total = total + jnp.where(send_idx[s] == w, live[s], 0.0) * send_grads[s]
        grad_out[w] = total
    for w in (0, 1, 3, 4):
        copy = remote(
            grad_out.at[w],
            grad_in.at[4 - w],
            grad_send.at[w],
            grad_recv.at[4 - w],
            offset(w - 2),
        )
        copy.start()
        pending.append(copy)
    for level in range(slots, rounds):
        ring_finish(level)
        if level + 1 < rounds:
            ring_start(level + 1)
    coord = grad_out[2]
    for w in (0, 1, 3, 4):
        remote(
            grad_out.at[w], grad_in.at[w], grad_send.at[w], grad_recv.at[w], offset(w - 2)
        ).wait_recv()
        coord = coord + grad_in[w]
    coord_ref[...] = coord
    adapter_ref[...] = ring_out[rounds]
    for copy in pending:
        copy.wait_send()


def finish(energy_in, coord_in, adapter_in, energy_ref, coord_ref, down_ref, up_ref):
    rank = up_ref.shape[0]
    energy_ref[...] = energy_in[...]
    coord_ref[...] = coord_in[0:3]
    down_ref[...] = jnp.transpose(adapter_in[0:rank])
    up_ref[...] = adapter_in[rank:]


def body(
    features,
    positions,
    species,
    block_pair_table,
    device_pair_count,
    edge_tile_masks,
    radial,
    element_scale_table,
    linear_mixing_weight,
    down_adapter_weight,
    up_adapter_weight,
    readout_weight,
    atom_energy_weight,
):
    count = lax.axis_size("space")
    rounds = count.bit_length() - 1
    assert count == 1 << rounds and rounds >= 3
    atoms, comps, channels = features.shape
    slots = edge_tile_masks.shape[0]
    basis = radial.shape[1]
    rank = up_adapter_weight.shape[0]
    vmem = pl.BlockSpec(memory_space=pltpu.VMEM)
    smem = pl.BlockSpec(memory_space=pltpu.SMEM)
    dma = pltpu.SemaphoreType.DMA
    block = (comps, atoms, channels)
    energy_row, coord_rows, adapter_rows = pl.pallas_call(
        functools.partial(kernel, count, rounds),
        out_shape=(
            jax.ShapeDtypeStruct((1, atoms), f32),
            jax.ShapeDtypeStruct((8, atoms), f32),
            jax.ShapeDtypeStruct((2 * rank, channels), f32),
        ),
        in_specs=[smem, smem] + [vmem] * 11,
        out_specs=(vmem,) * 3,
        scratch_shapes=[
            *[pltpu.VMEM((WINDOW, atoms, channels), bf16)] * comps,
            *[pltpu.VMEM((WINDOW, atoms, channels), f32)] * comps,
            pltpu.VMEM((WINDOW, 8, atoms), f32),
            pltpu.VMEM((WINDOW,) + block, f32),
            pltpu.VMEM((2,) + block, f32),
            pltpu.VMEM(block, f32),
            pltpu.VMEM(block, f32),
            pltpu.VMEM((slots, 4, basis, atoms, atoms), bf16),
            pltpu.VMEM((slots, basis, atoms, atoms), f32),
            pltpu.VMEM((slots, atoms, atoms), f32),
            pltpu.VMEM((slots, 3, atoms, atoms), f32),
            pltpu.VMEM((atoms, channels), f32),
            pltpu.VMEM((128, channels), f32),
            pltpu.VMEM((WINDOW, 8, atoms), f32),
            pltpu.VMEM((WINDOW, 8, atoms), f32),
            pltpu.VMEM((rounds + 1, 2 * rank, channels), f32),
            pltpu.VMEM((rounds, 2 * rank, channels), f32),
            dma((5, comps)),
            dma((WINDOW, comps)),
            dma((5, comps)),
            dma((WINDOW, comps)),
            dma((WINDOW,)),
            dma((WINDOW,)),
            dma((4, comps)),
            dma((4, comps)),
            dma((WINDOW,)),
            dma((WINDOW,)),
            dma((rounds,)),
            dma((rounds,)),
        ],
        compiler_params=pltpu.CompilerParams(
            collective_id=0, has_side_effects=True, vmem_limit_bytes=40 * 1024 * 1024
        ),
    )(
        block_pair_table,
        device_pair_count,
        jnp.transpose(features, (1, 0, 2)),
        positions,
        species.reshape(1, atoms),
        edge_tile_masks,
        radial,
        element_scale_table,
        linear_mixing_weight,
        down_adapter_weight,
        up_adapter_weight,
        readout_weight.reshape(1, channels),
        atom_energy_weight.reshape(1, atoms),
    )
    energies, coordinate_gradient, down_gradient, up_gradient = pl.pallas_call(
        finish,
        out_shape=(
            jax.ShapeDtypeStruct((1, atoms), f32),
            jax.ShapeDtypeStruct((3, atoms), f32),
            jax.ShapeDtypeStruct((channels, rank), f32),
            jax.ShapeDtypeStruct((rank, channels), f32),
        ),
    )(energy_row, coord_rows, adapter_rows)
    return (energies.reshape(atoms), coordinate_gradient, down_gradient, up_gradient)


def solution(mesh):
    placed = (
        P(("groups", "space"), None, None),
        P(None, ("groups", "space")),
        P(("groups", "space")),
        P(None, ("groups", "space")),
        P(("groups", "space")),
        P(("groups", "space"), None, None),
        P(),
        P(),
        P(),
        P(),
        P(),
        P(),
        P(("groups", "space")),
    )
    return jax.shard_map(
        body,
        mesh=mesh,
        in_specs=placed,
        out_specs=(
            P(("groups", "space")),
            P(None, ("groups", "space")),
            P("groups", None),
            P("groups", None),
        ),
        check_vma=False,
    )
```

```python
import functools

import jax
import jax.numpy as jnp
from jax import lax
from jax.experimental import pallas as pl
from jax.experimental.pallas import tpu as pltpu
from jax.sharding import PartitionSpec as P

REACH = 2
WINDOW = 2 * REACH + 1

soft_core = 0.25
centre_start = 1.0
highest = lax.Precision.HIGHEST
MESH = pl.DeviceIdType.MESH
FEAT_DIRECT = (0, 1, 2, 3)
MSG_DIRECT = (0,)
COT_DIRECT = (0,)
f32 = jnp.float32
bf16 = jnp.bfloat16


def dot(left, right):
    return jnp.dot(left, right, preferred_element_type=f32)


def dot_trailing(left, right):
    return lax.dot_general(left, right, (((1,), (1,)), ((), ())), preferred_element_type=f32)


def kernel(
    count,
    rounds,
    table_ref,
    live_ref,
    feat_ref,
    pos_ref,
    species_ref,
    mask_ref,
    radial_ref,
    scale_ref,
    mix_ref,
    down_ref,
    up_ref,
    readout_ref,
    weight_ref,
    energy_ref,
    coord_ref,
    down_grad_ref,
    up_grad_ref,
    feat_0,
    feat_1,
    feat_2,
    feat_3,
    agg_0,
    agg_1,
    agg_2,
    agg_3,
    pos_win,
    partial,
    sib_in,
    far_in,
    near_in,
    lefts,
    masked_buf,
    dist_buf,
    unit_buf,
    scale_buf,
    table_pad,
    grad_out,
    grad_in,
    ring_out,
    ring_in,
    feat_send,
    feat_recv,
    cot_send,
    cot_recv,
    pos_send,
    pos_recv,
    msg_send,
    msg_recv,
    grad_send,
    grad_recv,
    ring_send,
    ring_recv,
):
    comps, atoms, channels = feat_ref.shape
    feat_win = (feat_0, feat_1, feat_2, feat_3)
    agg_win = (agg_0, agg_1, agg_2, agg_3)
    slots = mask_ref.shape[0]
    basis = radial_ref.shape[1]
    me = lax.axis_index("space")
    core = lax.rem(me, 2)
    col = lax.rem(me // 2, 2)
    sib = me + 1 - 2 * core
    near = me + 2 - 4 * col
    far = lax.rem(me - 2 + 4 * col + count, count)
    onward = lax.rem(me + 4 - 8 * col + count, count)
    behind = lax.rem(me - 4 + 8 * col + count, count)
    near_slot = 4 - 4 * col
    far_slot = 4 * col
    sib_slot = 3 - 2 * core
    oth_slot = 1 + 2 * core
    through_slot = 4 - 4 * core

    def partner(level):
        step = 1 << level
        return me + step - 2 * step * lax.rem(me // step, 2)

    def offset(steps):
        return lax.rem(me + steps + count, count)

    def remote(src, dst, send, recv, device):
        return pltpu.make_async_remote_copy(
            src_ref=src,
            dst_ref=dst,
            send_sem=send,
            recv_sem=recv,
            device_id={"space": device},
            device_id_type=MESH,
        )

    barrier = pltpu.get_barrier_semaphore()
    greeted = [offset(steps) for steps in (-1, 1, -2, 2, -4, 4)]
    greeted += [partner(level) for level in range(3, rounds)]
    for device in greeted:
        pl.semaphore_signal(barrier, inc=1, device_id={"space": device}, device_id_type=MESH)

    for j in range(comps):
        feat_win[j][2] = feat_ref[j]
    pos_win[2] = jnp.zeros(pos_win.shape[1:], f32)
    pos_win[2, 0:3] = pos_ref[...]
    table_pad[...] = jnp.zeros(table_pad.shape, f32)
    table_pad[0 : scale_ref.shape[0]] = scale_ref[...]

    pl.semaphore_wait(barrier, len(greeted))

    def cast_copy(win, send, recv, kind, j):
        src, dst, device = (
            (2, far_slot, near),
            (2, oth_slot, sib),
            (near_slot, far_slot, onward),
            (through_slot, sib_slot, sib),
            (2, near_slot, far),
        )[kind]
        return remote(
            win[j].at[src], win[j].at[dst], send.at[kind, j], recv.at[dst, j], device
        )

    def cast_begin(win, send, recv, kind, j):
        copy = cast_copy(win, send, recv, kind, j)
        copy.start()
        pending.append(copy)

    def cast_start(win, send, recv, parts, direct):
        for j in parts:
            cast_begin(win, send, recv, 0, j)
            if j in direct:
                cast_begin(win, send, recv, 4, j)
        for j in parts:
            cast_begin(win, send, recv, 1, j)

    def arrived(win, send, recv, slot, j):
        remote(
            win[j].at[2], win[j].at[slot], send.at[0, j], recv.at[slot, j], near
        ).wait_recv()

    def cast_relay(win, send, recv, parts, direct):
        for j in parts:
            if j not in direct:
                arrived(win, send, recv, near_slot, j)
                cast_begin(win, send, recv, 2, j)

    def cast_forward(win, send, recv, parts, direct):
        for j in parts:
            if j in direct:
                arrived(win, send, recv, near_slot, j)
            arrived(win, send, recv, far_slot, j)
            cast_begin(win, send, recv, 3, j)

    def cast_finish(win, send, recv, parts):
        for j in parts:
            arrived(win, send, recv, sib_slot, j)
            arrived(win, send, recv, oth_slot, j)

    order = (1, 2, 3, 0)
    feat = (feat_win, feat_send, feat_recv)
    agg = (agg_win, cot_send, cot_recv)
    pending = []
    for w in (0, 1, 3, 4):
        copy = remote(
            pos_win.at[2],
            pos_win.at[4 - w],
            pos_send.at[w],
            pos_recv.at[4 - w],
            offset(w - 2),
        )
        copy.start()
        pending.append(copy)
    cast_start(*feat, range(comps), FEAT_DIRECT)

    species_cols = lax.broadcasted_iota(jnp.int32, (atoms, atoms), 0) == species_ref[...]
    one_hot = jnp.transpose(species_cols.astype(f32))
    scale_buf[...] = jnp.dot(
        one_hot, table_pad[...], precision=highest, preferred_element_type=f32
    )

    def window_of(block):
        return jnp.clip(lax.rem(block - me + REACH + 2 * count, count), 0, 2 * REACH)

    recv_idx = [window_of(table_ref[0, s]) for s in range(slots)]
    send_idx = [window_of(table_ref[1, s]) for s in range(slots)]
    live = [jnp.where(s < live_ref[0], 1.0, 0.0).astype(f32) for s in range(slots)]

    for w in (0, 1, 3, 4):
        remote(
            pos_win.at[2], pos_win.at[w], pos_send.at[w], pos_recv.at[w], offset(w - 2)
        ).wait_recv()

    cast_relay(*feat, range(comps), FEAT_DIRECT)

    for s in range(slots):
        columns = jnp.transpose(pos_win[recv_idx[s]])
        rows = pos_win[send_idx[s]]
        offsets = [rows[x : x + 1, :] - columns[:, x : x + 1] for x in range(3)]
        dist = jnp.sqrt(
            offsets[0] * offsets[0] + offsets[1] * offsets[1] + offsets[2] * offsets[2] + soft_core
        )
        inverse = 1.0 / dist
        dist_buf[s] = dist
        for x in range(3):
            unit_buf[s, x] = offsets[x] * inverse

        def build(k, carry, s=s):
            scaled = dist_buf[s] - (centre_start + k.astype(f32))
            masked = jnp.exp(-scaled * scaled) * mask_ref[s].astype(f32)
            masked_buf[s, k] = masked
            lefts[s, 0, k] = masked.astype(bf16)
            for x in range(3):
                lefts[s, 1 + x, k] = (masked * unit_buf[s, x]).astype(bf16)
            return carry

        lax.fori_loop(0, basis, build, 0)

    cast_forward(*feat, (0, 1), FEAT_DIRECT)
    cast_finish(*feat, (0, 1))

    share = [
        [jnp.where(recv_idx[s] == w, live[s], 0.0) for s in range(slots)] for w in range(WINDOW)
    ]

    def weighted(product, path):
        total = radial_ref[path, 0:1, :] * product[0:atoms]
        for k in range(1, basis):
            total = total + radial_ref[path, k : k + 1, :] * product[k * atoms : (k + 1) * atoms]
        return total

    def component(j):
        terms = []
        for s in range(slots):
            plain = lefts[s, 0].reshape(basis * atoms, atoms)
            straight = dot(plain, feat_win[j][send_idx[s]])
            if j == 0:
                turned = [lefts[s, 1 + x].reshape(basis * atoms, atoms) for x in range(3)]
                tall = jnp.concatenate([feat_win[1 + x][send_idx[s]] for x in range(3)], axis=0)
                crossed = dot(jnp.concatenate(turned, axis=1), tall)
                terms.append(weighted(straight, 0) + weighted(crossed, 1))
            else:
                turned = lefts[s, j].reshape(basis * atoms, atoms)
                crossed = dot(turned, feat_win[0][send_idx[s]])
                terms.append(weighted(crossed, 2) + weighted(straight, 3))
        for w in range(WINDOW):
            total = share[w][0] * terms[0]
            for s in range(1, slots):
                total = total + share[w][s] * terms[s]
            partial[w, j] = total

    def message_copy(hop, j):
        src, dst, device = (
            (partial.at[oth_slot, j], sib_in.at[0, j], sib),
            (partial.at[sib_slot, j], sib_in.at[1, j], sib),
            (partial.at[far_slot, j], far_in.at[j], far if j in MSG_DIRECT else behind),
            (partial.at[near_slot, j], near_in.at[j], near),
        )[hop]
        return remote(src, dst, msg_send.at[hop, j], msg_recv.at[hop, j], device)

    def message_start(hop, j):
        copy = message_copy(hop, j)
        copy.start()
        pending.append(copy)

    def to_sib(j):
        component(j)
        message_start(0, j)
        message_start(1, j)

    def to_far(j):
        message_copy(0, j).wait_recv()
        partial[through_slot, j] += sib_in[0, j]
        message_start(2, j)

    def to_near(j):
        if j not in MSG_DIRECT:
            message_copy(2, j).wait_recv()
            partial[near_slot, j] += far_in[j]
        message_start(3, j)

    def gather(j):
        message_copy(1, j).wait_recv()
        total = partial[2, j] + sib_in[1, j]
        if j in MSG_DIRECT:
            message_copy(2, j).wait_recv()
            total = total + far_in[j]
        message_copy(3, j).wait_recv()
        return total + near_in[j]

    to_sib(1)
    cast_forward(*feat, (2,), FEAT_DIRECT)
    cast_finish(*feat, (2,))
    to_sib(2)
    to_far(1)
    cast_forward(*feat, (3,), FEAT_DIRECT)
    cast_finish(*feat, (3,))
    to_sib(3)
    to_far(2)
    to_sib(0)
    to_near(1)
    to_far(3)
    to_far(0)
    if 0 in MSG_DIRECT:
        to_near(0)
    to_near(2)
    to_near(3)
    if 0 not in MSG_DIRECT:
        to_near(0)
    for j in (1, 2, 3):
        agg_win[j][2] = gather(j)
        cast_start(*agg, (j,), COT_DIRECT)
    cast_relay(*agg, (1,), COT_DIRECT)
    gathered = [gather(0)] + [agg_win[j][2] for j in (1, 2, 3)]

    scale = scale_buf[...]
    squares = gathered[1] * gathered[1] + gathered[2] * gathered[2] + gathered[3] * gathered[3]
    invariant = (scale * (gathered[0] + squares)).astype(bf16)
    low_rank = dot(invariant, down_ref[...]).astype(bf16)
    hidden = dot(invariant, mix_ref[...]) + dot(low_rank, up_ref[...])
    sigma = jax.nn.sigmoid(hidden)
    weight_cols = jnp.transpose(jnp.broadcast_to(weight_ref[...], (atoms, atoms)))
    if channels != atoms:
        weight_cols = jnp.broadcast_to(weight_cols[:, :1], (atoms, channels))
    slope = sigma * (1.0 + hidden * (1.0 - sigma))
    grad_pre = (weight_cols * readout_ref[...] * slope).astype(bf16)
    grad_low = dot_trailing(grad_pre, up_ref[...]).astype(bf16)
    grad_inv = dot_trailing(grad_pre, mix_ref[...]) + dot_trailing(grad_low, down_ref[...])
    seed = scale * grad_inv
    agg_win[0][2] = seed
    cast_start(*agg, (0,), COT_DIRECT)
    cast_relay(*agg, (2, 3, 0), COT_DIRECT)

    rank = up_ref.shape[0]
    ring_out[0, 0:rank] = dot(jnp.transpose(grad_low.astype(f32)).astype(bf16), invariant)
    ring_out[0, rank:] = dot(jnp.transpose(low_rank.astype(f32)).astype(bf16), grad_pre)
    energy_ref[...] = jnp.sum(
        jnp.transpose(hidden * sigma * readout_ref[...]), axis=0, keepdims=True
    )

    def ring_copy(level):
        return remote(
            ring_out.at[level],
            ring_in.at[level],
            ring_send.at[level],
            ring_recv.at[level],
            partner(level),
        )

    def ring_start(level):
        copy = ring_copy(level)
        copy.start()
        pending.append(copy)

    def ring_finish(level):
        ring_copy(level).wait_recv()
        ring_out[level + 1] = ring_out[level] + ring_in[level]

    ring_start(0)
    ring_finish(0)
    ring_start(1)
    cast_forward(*agg, order, COT_DIRECT)
    cast_finish(*agg, order)

    lanes = lax.broadcasted_iota(jnp.int32, (atoms, atoms), 1)
    row_ids = lax.broadcasted_iota(jnp.int32, (8, atoms), 0)
    recv_grads, send_grads = [], []
    for s in range(slots):
        sent = [feat_win[j][send_idx[s]] for j in range(4)]
        wide = jnp.concatenate(sent, axis=1)
        pairs = [jnp.concatenate([sent[0], sent[1 + x]], axis=1) for x in range(3)]

        cot = [agg_win[0][recv_idx[s]]]
        for x in range(3):
            cot.append(2.0 * cot[0] * agg_win[1 + x][recv_idx[s]])
        gap = dist_buf[s]
        units = [unit_buf[s, x] for x in range(3)]
        grad_dist = jnp.zeros((atoms, atoms), f32)
        dirs = [jnp.zeros((atoms, atoms), f32) for x in range(3)]
        for k in range(basis):
            weight = [radial_ref[path, k : k + 1, :] for path in range(4)]
            wall = jnp.concatenate(
                [(weight[0] * cot[0]).astype(bf16)]
                + [(weight[3] * cot[1 + x]).astype(bf16) for x in range(3)],
                axis=1,
            )
            inner = (weight[1] * cot[0]).astype(bf16)
            total = dot_trailing(wall, wide)
            masked = masked_buf[s, k]
            for x in range(3):
                along = (weight[2] * cot[1 + x]).astype(bf16)
                grad_dir = dot_trailing(jnp.concatenate([along, inner], axis=1), pairs[x])
                total = total + grad_dir * units[x]
                dirs[x] = dirs[x] + masked * grad_dir
            grad_dist = grad_dist + total * masked * (-2.0 * (gap - (centre_start + k)))
        radial_part = dirs[0] * units[0] + dirs[1] * units[1] + dirs[2] * units[2]
        inverse = 1.0 / gap
        columns = jnp.zeros((atoms, atoms), f32)
        send_rows = jnp.zeros((8, atoms), f32)
        for x in range(3):
            grad = grad_dist * units[x] + (dirs[x] - units[x] * radial_part) * inverse
            columns = jnp.where(lanes == x, jnp.sum(grad, axis=1, keepdims=True), columns)
            send_rows = jnp.where(row_ids == x, jnp.sum(grad, axis=0, keepdims=True), send_rows)
        recv_grads.append(-jnp.transpose(columns)[0:8])
        send_grads.append(send_rows)
        if s + 1 < min(rounds, slots):
            ring_finish(s + 1)
            ring_start(s + 2)

    for w in range(WINDOW):
        total = jnp.zeros((8, atoms), f32)
        for s in range(slots):
            total = total + share[w][s] * recv_grads[s]
            total = total + jnp.where(send_idx[s] == w, live[s], 0.0) * send_grads[s]
        grad_out[w] = total
    for w in (0, 1, 3, 4):
        copy = remote(
            grad_out.at[w],
            grad_in.at[4 - w],
            grad_send.at[w],
            grad_recv.at[4 - w],
            offset(w - 2),
        )
        copy.start()
        pending.append(copy)
    for level in range(slots, rounds):
        ring_finish(level)
        if level + 1 < rounds:
            ring_start(level + 1)
    coord = grad_out[2]
    for w in (0, 1, 3, 4):
        remote(
            grad_out.at[w], grad_in.at[w], grad_send.at[w], grad_recv.at[w], offset(w - 2)
        ).wait_recv()
        coord = coord + grad_in[w]
    coord_ref[...] = coord[0:3]
    down_grad_ref[...] = ring_out[rounds, 0:rank]
    up_grad_ref[...] = ring_out[rounds, rank:]
    for copy in pending:
        copy.wait_send()


def body(
    features,
    positions,
    species,
    block_pair_table,
    device_pair_count,
    edge_tile_masks,
    radial,
    element_scale_table,
    linear_mixing_weight,
    down_adapter_weight,
    up_adapter_weight,
    readout_weight,
    atom_energy_weight,
):
    count = lax.axis_size("space")
    rounds = count.bit_length() - 1
    assert count == 1 << rounds and rounds >= 3
    atoms, comps, channels = features.shape
    slots = edge_tile_masks.shape[0]
    basis = radial.shape[1]
    rank = up_adapter_weight.shape[0]
    vmem = pl.BlockSpec(memory_space=pltpu.VMEM)
    smem = pl.BlockSpec(memory_space=pltpu.SMEM)
    dma = pltpu.SemaphoreType.DMA
    block = (comps, atoms, channels)
    energies, coordinate_gradient, down_gradient, up_gradient = pl.pallas_call(
        functools.partial(kernel, count, rounds),
        out_shape=(
            jax.ShapeDtypeStruct((1, atoms), f32),
            jax.ShapeDtypeStruct((3, atoms), f32),
            jax.ShapeDtypeStruct((rank, channels), f32),
            jax.ShapeDtypeStruct((rank, channels), f32),
        ),
        in_specs=[smem, smem] + [vmem] * 11,
        out_specs=(vmem,) * 4,
        scratch_shapes=[
            *[pltpu.VMEM((WINDOW, atoms, channels), bf16)] * comps,
            *[pltpu.VMEM((WINDOW, atoms, channels), f32)] * comps,
            pltpu.VMEM((WINDOW, 8, atoms), f32),
            pltpu.VMEM((WINDOW,) + block, f32),
            pltpu.VMEM((2,) + block, f32),
            pltpu.VMEM(block, f32),
            pltpu.VMEM(block, f32),
            pltpu.VMEM((slots, 4, basis, atoms, atoms), bf16),
            pltpu.VMEM((slots, basis, atoms, atoms), f32),
            pltpu.VMEM((slots, atoms, atoms), f32),
            pltpu.VMEM((slots, 3, atoms, atoms), f32),
            pltpu.VMEM((atoms, channels), f32),
            pltpu.VMEM((128, channels), f32),
            pltpu.VMEM((WINDOW, 8, atoms), f32),
            pltpu.VMEM((WINDOW, 8, atoms), f32),
            pltpu.VMEM((rounds + 1, 2 * rank, channels), f32),
            pltpu.VMEM((rounds, 2 * rank, channels), f32),
            dma((5, comps)),
            dma((WINDOW, comps)),
            dma((5, comps)),
            dma((WINDOW, comps)),
            dma((WINDOW,)),
            dma((WINDOW,)),
            dma((4, comps)),
            dma((4, comps)),
            dma((WINDOW,)),
            dma((WINDOW,)),
            dma((rounds,)),
            dma((rounds,)),
        ],
        compiler_params=pltpu.CompilerParams(
            collective_id=0, has_side_effects=True, vmem_limit_bytes=40 * 1024 * 1024
        ),
    )(
        block_pair_table,
        device_pair_count,
        jnp.transpose(features, (1, 0, 2)),
        positions,
        species.reshape(1, atoms),
        edge_tile_masks,
        radial,
        element_scale_table,
        linear_mixing_weight,
        down_adapter_weight,
        up_adapter_weight,
        readout_weight.reshape(1, channels),
        atom_energy_weight.reshape(1, atoms),
    )
    return (
        energies.reshape(atoms),
        coordinate_gradient,
        jnp.transpose(down_gradient),
        up_gradient,
    )


def solution(mesh):
    placed = (
        P(("groups", "space"), None, None),
        P(None, ("groups", "space")),
        P(("groups", "space")),
        P(None, ("groups", "space")),
        P(("groups", "space")),
        P(("groups", "space"), None, None),
        P(),
        P(),
        P(),
        P(),
        P(),
        P(),
        P(("groups", "space")),
    )
    return jax.shard_map(
        body,
        mesh=mesh,
        in_specs=placed,
        out_specs=(
            P(("groups", "space")),
            P(None, ("groups", "space")),
            P("groups", None),
            P("groups", None),
        ),
        check_vma=False,
    )
```
